128 devices in a mesh: dp: 2 (over x_hi), blk: 64 (over x_lo, y, z, core).
Axes of the slice: x: 4 (x_hi: 2, x_lo: 2; x = x_hi * 2 + x_lo), y: 4, z: 4, core: 2. Of those that a mesh axis runs over, the one named last changes fastest.
Arguments:
- queries: bfloat16 [32768, 2048], P(('dp', 'blk')), parts along dimension 0, may hold values from -8 to 8
- key_rows: bfloat16 [32768, 2048], P(('dp', 'blk')), parts along dimension 0, may hold values from -8 to 8
- value_rows: bfloat16 [32768, 2048], P(('dp', 'blk')), parts along dimension 0, may hold values from -6 to 6
- out_grad: bfloat16 [32768, 2048], P(('dp', 'blk')), parts along dimension 0, may hold values from -6 to 6
- doc_lengths: int32 [32], P('dp'), parts along dimension 0, may hold values from 1 to 1536, 16384 in all
Outputs:
- attended: bfloat16 [32768, 2048], P(('dp', 'blk')), parts along dimension 0
- query_grad: bfloat16 [32768, 2048], P(('dp', 'blk')), parts along dimension 0
- key_grad: bfloat16 [32768, 2048], P(('dp', 'blk')), parts along dimension 0
- value_grad: bfloat16 [32768, 2048], P(('dp', 'blk')), parts along dimension 0
The draws below stay inside these ranges and needn't reach their ends.
There are 2 independent parts, one for each index of `dp`. The reference program is written for one: setup_inputs(seed, part) draws one part's arguments, and reference() takes and returns one part's arrays. A program takes and returns all parts, laid end to end along the dimension named above; each array names one. Nothing has to cross between parts.
Inputs may be any that keep to these rules, and one draw needn't show every extreme that they name: `doc_lengths`: the lengths sum to 16384; the longest document has exactly 1536 tokens.
All inputs are finite; a program needn't handle non-finite values.
Results may differ from the reference program's by a relative error of at most 0.011.
Values may be sent and summed in bfloat16 or wider, within the bound.
A program may use at most 192 MiB of HBM per device.

```python
import math
import jax
import jax.numpy as jnp
import numpy as np
from jax import lax

HEADS = 16
HEAD_DIM = 128
TOK_DEV = 256
REACH = 6
MAXDOC = 1536
NDOCS = 16
TOKENS = 16384
N_BLK = 64


def draw_queries(key, part):
    key = jax.random.fold_in(key, 11)
    values = jnp.clip(jax.random.normal(key, (TOKENS, HEADS * HEAD_DIM)), -8.0, 8.0)
    return values.astype(jnp.bfloat16)


def draw_key_rows(key, part):
    key = jax.random.fold_in(key, 23)
    values = jnp.clip(jax.random.normal(key, (TOKENS, HEADS * HEAD_DIM)), -8.0, 8.0)
    return values.astype(jnp.bfloat16)


def shard_levels(rng, dims, shards, least, top_value):
    def one(axis_at, parts):
        heights = jax.random.uniform(jax.random.fold_in(jax.random.fold_in(rng, 6), axis_at), (parts,), jnp.float32, least / len(shards), top_value / len(shards))
        return jnp.repeat(jnp.exp(heights), dims[axis_at] // parts).reshape((-1,) + (1,) * (len(dims) - axis_at - 1))

    factor_of = one(*shards[0])
    for cut in shards[1:]:
        factor_of = factor_of * one(*cut)
    return factor_of


def profile(amount, total, reach, skew):
    weights = [(1 << 20) // math.isqrt(grade ** skew) + 1 for grade in range(2, amount + 1)]
    surplus, given = total - reach - (amount - 1), [1] * (amount - 1)
    while surplus > 0:
        candidates = [i for i in range(amount - 1) if given[i] < reach]
        mass, budget = sum([weights[i] for i in candidates]), surplus
        for i in candidates:
            more = min(reach - given[i], max(1, budget * weights[i] // mass), surplus)
            given[i] = given[i] + more
            surplus = surplus - more
    return np.array([reach] + given)


def ragged(key, count, total, limit, skew):
    if count == 2:
        one = jax.random.randint(key, (), max(1, total - limit), min(limit, total - 1) + 1)
        return jnp.stack([one, total - one])
    lengths = jnp.asarray(profile(count, total, limit, skew), jnp.int32)
    twos = (count - 1) // 2
    source_of, taker = lengths[1:1 + 2 * twos:2], lengths[2:2 + 2 * twos:2]
    room = jnp.minimum(source_of - 1, limit - taker)
    passed = jax.random.randint(jax.random.fold_in(key, 1), (twos,), 0, 1 << 20) % (room + 1)
    lengths = lengths.at[1:1 + 2 * twos:2].set(source_of - passed).at[2:2 + 2 * twos:2].set(taker + passed)
    return lengths[jax.random.permutation(jax.random.fold_in(key, 2), count)]


def normal_values(rng, dims, spread, most, cuts=(), held_as=jnp.bfloat16):
    result = spread * jax.random.normal(rng, dims, jnp.float32)
    if cuts:
        result = result * shard_levels(rng, dims, cuts, -0.22, 0.18)
    return jnp.clip(result, -most, most).astype(held_as)


def setup_inputs(seed: int = 0, part: int = 0) -> dict:
    key_list = jax.random.split(jax.random.key(seed), 6)
    part_keys = jax.random.split(jax.random.fold_in(key_list[5], part), 6)
    return {
        "queries": draw_queries(jax.random.fold_in(jax.random.fold_in(key_list[5], part), 71), part),
        "key_rows": draw_key_rows(jax.random.fold_in(jax.random.fold_in(key_list[5], part), 71), part),
        "value_rows": normal_values(part_keys[2], (TOKENS, HEADS * HEAD_DIM), 1.0, 6.0, ((0, 64),)),
        "out_grad": normal_values(part_keys[3], (TOKENS, HEADS * HEAD_DIM), 1.0, 6.0, ((0, 64),)),
        "doc_lengths": ragged(part_keys[4], NDOCS, TOKENS, MAXDOC, 1).astype(jnp.int32),
    }


NEG_FILL = -1e+30

def document_index(doc_lengths, positions):
    doc_ends = jnp.cumsum(doc_lengths)
    return lax.optimization_barrier(jnp.sum((doc_ends[None, :] <= positions[:, None]).astype(jnp.int32), axis=1))

def reference(queries, key_rows, value_rows, out_grad, doc_lengths):
    shard_rows = TOK_DEV
    margin = REACH * TOK_DEV
    window = (REACH + 1) * TOK_DEV
    feature_width = HEADS * HEAD_DIM
    scale_factor = 1.0 / math.sqrt(HEAD_DIM)
    zero_rows = jnp.zeros((margin, feature_width), jnp.bfloat16)
    keys_padded = jnp.concatenate([zero_rows, key_rows], axis=0)
    values_padded = jnp.concatenate([zero_rows, value_rows], axis=0)

    def split_heads(matrix):
        return matrix.astype(jnp.float32).reshape(matrix.shape[0], HEADS, HEAD_DIM)

    def visit_block(accumulators, block_number):
        key_accum, value_accum = accumulators
        row_start = (block_number * shard_rows).astype(jnp.int32)
        query_block = lax.dynamic_slice_in_dim(queries, row_start, shard_rows, 0)
        grad_block = lax.dynamic_slice_in_dim(out_grad, row_start, shard_rows, 0)
        key_window = lax.dynamic_slice_in_dim(keys_padded, row_start, window, 0)
        value_window = lax.dynamic_slice_in_dim(values_padded, row_start, window, 0)
        query_pos = row_start + jnp.arange(shard_rows, dtype=jnp.int32)
        key_pos = row_start - margin + jnp.arange(window, dtype=jnp.int32)
        same_doc = document_index(doc_lengths, key_pos)[None, :] == document_index(doc_lengths, query_pos)[:, None]
        allowed = same_doc & (key_pos[None, :] <= query_pos[:, None]) & (key_pos[None, :] >= 0)
        query_heads = split_heads(query_block)
        key_heads = split_heads(key_window)
        value_heads = split_heads(value_window)
        grad_heads = split_heads(grad_block)
        scores = jnp.einsum('thd,khd->htk', query_heads, key_heads) * scale_factor
        scores = jnp.where(allowed[None], scores, NEG_FILL)
        row_max = lax.optimization_barrier(jnp.max(scores, axis=2, keepdims=True))
        log_total = row_max + jnp.log(lax.optimization_barrier(jnp.sum(jnp.exp(scores - row_max), axis=2, keepdims=True)))
        weights = jnp.where(allowed[None], jnp.exp(scores - log_total), 0.0)
        weights_low = lax.optimization_barrier(weights.astype(jnp.bfloat16)).astype(jnp.float32)
        attended = jnp.einsum('htk,khd->thd', weights_low, value_heads).reshape(shard_rows, feature_width).astype(jnp.bfloat16)
        row_delta = lax.optimization_barrier(jnp.sum(grad_heads * split_heads(attended), axis=2)).T[:, :, None]
        weight_grads = jnp.einsum('thd,khd->htk', grad_heads, value_heads)
        score_grads = weights * (weight_grads - row_delta) * scale_factor
        score_low = lax.optimization_barrier(score_grads.astype(jnp.bfloat16)).astype(jnp.float32)
        query_grads = jnp.einsum('htk,khd->thd', score_low, key_heads).reshape(shard_rows, feature_width).astype(jnp.bfloat16)
        key_part = jnp.einsum('htk,thd->khd', score_low, query_heads).reshape(window, feature_width)
        value_part = jnp.einsum('htk,thd->khd', weights_low, grad_heads).reshape(window, feature_width)
        key_accum = lax.dynamic_update_slice_in_dim(key_accum, lax.dynamic_slice_in_dim(key_accum, row_start, window, 0) + key_part, row_start, 0)
        value_accum = lax.dynamic_update_slice_in_dim(value_accum, lax.dynamic_slice_in_dim(value_accum, row_start, window, 0) + value_part, row_start, 0)
        return ((key_accum, value_accum), (attended, query_grads))
    empty_grads = jnp.zeros((TOKENS + margin, feature_width), jnp.float32)
    (key_accum, value_accum), (attended, query_grads) = lax.scan(visit_block, (empty_grads, empty_grads), jnp.arange(N_BLK, dtype=jnp.int32))
    return (attended.reshape(TOKENS, feature_width), query_grads.reshape(TOKENS, feature_width), key_accum[margin:].astype(jnp.bfloat16), value_accum[margin:].astype(jnp.bfloat16))
```

```python
import functools
import math

import jax
import jax.numpy as jnp
from jax import lax
from jax.experimental import pallas as pl
from jax.experimental.pallas import tpu as pltpu
from jax.sharding import PartitionSpec as P

HEAD_DIM = 128
REACH = 6
RING = 8
HEADS_EACH = 2
NEG_FILL = -1e30
SCALE = 1.0 / math.sqrt(HEAD_DIM)
SCALE_LOG2 = SCALE * math.log2(math.e)
MESH = pl.DeviceIdType.MESH


def dot_nt(a, b):
    return lax.dot_general(a, b, (((1,), (1,)), ((), ())), preferred_element_type=jnp.float32)


def dot_nn(a, b):
    return jnp.dot(a, b, preferred_element_type=jnp.float32)


def kernel(
    n_blk, tok,
    doc_lengths, q_in, k_in, v_in, g_in,
    o_out, dq_out, dk_out, dv_out,
    k_buf, v_buf, q_buf, g_buf, kt, vt, start_ref,
    s_ref, d_ref, p_ref, ds_ref, acc_k, acc_v,
    o_stage, kv_stage, halo_send, halo_recv,
    in_send, in_recv, fwd_send, fwd_recv, back_send, back_recv, out_send, out_recv,
):
    me = lax.axis_index("blk")
    group, rank = me // RING, lax.rem(me, RING)
    n_groups = n_blk // RING
    window = (REACH + 1) * tok
    halo = REACH * tok

    def ring_device(member):
        return {"blk": group * RING + member}

    next_device = {"blk": lax.rem(group + 1, n_groups) * RING + rank}
    prev_device = {"blk": lax.rem(group + n_groups - 1, n_groups) * RING + rank}

    def member(k):
        return lax.rem(rank + k + RING, RING)

    def head_cols(owner, hh):
        return pl.ds(pl.multiple_of((owner * HEADS_EACH + hh) * HEAD_DIM, HEAD_DIM), HEAD_DIM)

    def rows(shard):
        return pl.ds(pl.multiple_of(shard * tok, tok), tok)

    def landed(ref, sem):
        pltpu.make_async_copy(ref, ref, sem).wait()

    sources = (k_in, v_in, q_in, g_in)

    def slot(hh, a, shard):
        if a < 2:
            return (k_buf, v_buf)[a].at[hh, rows(shard + REACH), :]
        return (q_buf, g_buf)[a - 2].at[hh, rows(shard), :]

    def in_copy(hh, a, target):
        return pltpu.make_async_remote_copy(
            src_ref=sources[a].at[:, head_cols(target, hh)],
            dst_ref=slot(hh, a, rank),
            send_sem=in_send.at[hh, a, target],
            recv_sem=in_recv.at[hh, a, rank],
            device_id=ring_device(target),
            device_id_type=MESH,
        )

    def own_copy(hh, a):
        return pltpu.make_async_copy(
            sources[a].at[:, head_cols(rank, hh)], slot(hh, a, rank), in_recv.at[hh, a, rank]
        )

    def in_landed(hh, a, shard):
        landed(slot(hh, a, shard), in_recv.at[hh, a, shard])

    def fwd_copy(hh, a, shard):
        h = shard - (RING - REACH)
        return pltpu.make_async_remote_copy(
            src_ref=slot(hh, a, shard),
            dst_ref=(k_buf, v_buf)[a].at[hh, rows(h), :],
            send_sem=fwd_send.at[hh, a, h],
            recv_sem=fwd_recv.at[hh, a, h],
            device_id=next_device,
            device_id_type=MESH,
        )

    def forward(hh, shard):
        for a in range(2):
            in_landed(hh, a, shard)

        @pl.when(shard >= RING - REACH)
        def _():
            for a in range(2):
                fwd_copy(hh, a, shard).start()

    def back_copy(hh, a, h):
        return pltpu.make_async_remote_copy(
            src_ref=halo_send.at[hh, a, rows(h), :],
            dst_ref=halo_recv.at[hh, a, rows(h), :],
            send_sem=back_send.at[hh, a, h],
            recv_sem=back_recv.at[hh, a, h],
            device_id=prev_device,
            device_id_type=MESH,
        )

    results = (o_out, dq_out, dk_out, dv_out)

    def staged(hh, a, shard):
        if a < 2:
            return o_stage.at[hh, a, rows(shard), :]
        return kv_stage.at[hh, a - 2, rows(shard), :]

    def out_copy(hh, a, target):
        return pltpu.make_async_remote_copy(
            src_ref=staged(hh, a, target),
            dst_ref=results[a].at[:, head_cols(rank, hh)],
            send_sem=out_send.at[hh, a, target],
            recv_sem=out_recv.at[hh, a, rank],
            device_id=ring_device(target),
            device_id_type=MESH,
        )

    def send_results(hh, first, target):
        @pl.when(target != rank)
        def _():
            for a in (first, first + 1):
                out_copy(hh, a, target).start()

        @pl.when(target == rank)
        def _():
            for a in (first, first + 1):
                pltpu.make_async_copy(
                    staged(hh, a, target),
                    results[a].at[:, head_cols(rank, hh)],
                    out_recv.at[hh, a, rank],
                ).start()

    barrier = pltpu.get_barrier_semaphore()
    for k in range(1, RING):
        pl.semaphore_signal(barrier, inc=1, device_id=ring_device(member(k)), device_id_type=MESH)
    pl.semaphore_signal(barrier, inc=1, device_id=next_device, device_id_type=MESH)
    pl.semaphore_signal(barrier, inc=1, device_id=prev_device, device_id_type=MESH)
    pl.semaphore_wait(barrier, RING + 1)

    def start_kv0(k, _):
        for a in (0, 1):
            in_copy(0, a, member(k)).start()
        return 0

    lax.fori_loop(1, RING, start_kv0, 0)
    for hh in range(HEADS_EACH):
        for a in range(4):
            own_copy(hh, a).start()

    position = group * RING * tok + (
        lax.broadcasted_iota(jnp.int32, (RING, tok), 0) * tok
        + lax.broadcasted_iota(jnp.int32, (RING, tok), 1)
    )
    first_key = jnp.zeros((RING, tok), jnp.int32)
    doc_end = jnp.int32(0)
    for j in range(doc_lengths.shape[0]):
        doc_end = doc_end + doc_lengths[j]
        first_key = jnp.where(position >= doc_end, doc_end, first_key)
    window_base = group * RING * tok - halo + lax.broadcasted_iota(jnp.int32, (RING, tok), 0) * tok
    start_ref[...] = first_key - window_base

    forward(0, rank)

    def start_qg0(k, _):
        target = member(k)
        for a in (0, 1):
            in_copy(0, a, target).wait_send()
        for a in (2, 3):
            in_copy(0, a, target).start()
        forward(0, member(-k))
        return 0

    lax.fori_loop(1, RING, start_qg0, 0)

    def start_kv1(k, _):
        target = member(k)
        for a in (2, 3):
            in_copy(0, a, target).wait_send()
        for a in (0, 1):
            in_copy(1, a, target).start()
        return 0

    lax.fori_loop(1, RING, start_kv1, 0)
    forward(1, rank)

    def transposed(hh, shard):
        kt[:, rows(shard)] = k_buf[hh, rows(shard), :].T
        vt[:, rows(shard)] = v_buf[hh, rows(shard), :].T

    key_row = lax.broadcasted_iota(jnp.int32, (tok, tok), 0)
    query_col = lax.broadcasted_iota(jnp.int32, (tok, tok), 1)

    def attend(hh, i):
        win = pl.ds(pl.multiple_of(i * tok, tok), window)
        q = q_buf[hh, rows(i), :]
        g = g_buf[hh, rows(i), :]
        start = start_ref[pl.ds(i, 1), :]
        s_ref[...] = dot_nt(k_buf[hh, win, :], q)
        top = None
        for b in range(REACH + 1):
            block = pl.ds(b * tok, tok)
            allowed = key_row >= start - b * tok
            if b == REACH:
                allowed = allowed & (key_row <= query_col)
            s = jnp.where(allowed, s_ref[block, :], NEG_FILL)
            s_ref[block, :] = s
            block_top = jnp.max(s, axis=0, keepdims=True)
            top = block_top if top is None else jnp.maximum(top, block_top)
        top = top * SCALE_LOG2
        total = None
        for b in range(REACH + 1):
            block = pl.ds(b * tok, tok)
            p = jnp.exp2(s_ref[block, :] * SCALE_LOG2 - top)
            s_ref[block, :] = p
            block_total = jnp.sum(p, axis=0, keepdims=True)
            total = block_total if total is None else total + block_total
        inverse = 1.0 / total
        for b in range(REACH + 1):
            block = pl.ds(b * tok, tok)
            p = s_ref[block, :] * inverse
            s_ref[block, :] = p
            p_ref[block, :] = p.astype(jnp.bfloat16)
        attended = dot_nn(vt[:, win], p_ref[...]).astype(jnp.bfloat16)
        o_stage[hh, 0, rows(i), :] = attended.T
        delta = jnp.sum(
            attended.astype(jnp.float32) * g.T.astype(jnp.float32), axis=0, keepdims=True
        )
        d_ref[...] = dot_nt(v_buf[hh, win, :], g)
        for b in range(REACH + 1):
            block = pl.ds(b * tok, tok)
            ds_ref[block, :] = (s_ref[block, :] * (d_ref[block, :] - delta)).astype(jnp.bfloat16)
        dq = dot_nn(kt[:, win], ds_ref[...]) * SCALE
        acc_k[win, :] += dot_nn(ds_ref[...], q)
        acc_v[win, :] += dot_nn(p_ref[...], g)
        o_stage[hh, 1, rows(i), :] = dq.astype(jnp.bfloat16).T

    def step(t, _):
        hh, i = t // RING, lax.rem(t, RING)

        @pl.when(i == 0)
        def _():
            acc_k[...] = jnp.zeros_like(acc_k)
            acc_v[...] = jnp.zeros_like(acc_v)

            def one(h, _):
                landed(k_buf.at[hh, rows(h), :], fwd_recv.at[hh, 0, h])
                landed(v_buf.at[hh, rows(h), :], fwd_recv.at[hh, 1, h])
                transposed(hh, h)
                return 0

            lax.fori_loop(0, REACH, one, 0)

        @pl.when((t >= 1) & (t < RING))
        def _():
            target = member(t)
            for a in (0, 1):
                in_copy(1, a, target).wait_send()
            for a in (2, 3):
                in_copy(1, a, target).start()
            forward(1, member(-t))

        for a in (2, 3):
            in_landed(hh, a, i)
        transposed(hh, i + REACH)
        attend(hh, i)
        send_results(hh, 0, i)

        @pl.when(i < REACH)
        def _():
            halo_send[hh, 0, rows(i), :] = (acc_k[rows(i), :] * SCALE).astype(jnp.bfloat16)
            halo_send[hh, 1, rows(i), :] = acc_v[rows(i), :].astype(jnp.bfloat16)
            for a in range(2):
                back_copy(hh, a, i).start()

        @pl.when(i == RING - 1)
        def _():
            def finish(shard, _):
                def put(dk, dv):
                    kv_stage[hh, 0, rows(shard), :] = dk.astype(jnp.bfloat16)
                    kv_stage[hh, 1, rows(shard), :] = dv.astype(jnp.bfloat16)

                own = rows(shard + REACH)

                @pl.when(shard < RING - REACH)
                def _():
                    put(acc_k[own, :] * SCALE, acc_v[own, :])

                @pl.when(shard >= RING - REACH)
                def _():
                    h = shard - (RING - REACH)
                    for a in range(2):
                        landed(halo_recv.at[hh, a, rows(h), :], back_recv.at[hh, a, h])
                    put(
                        acc_k[own, :] * SCALE + halo_recv[hh, 0, rows(h), :].astype(jnp.float32),
                        acc_v[own, :] + halo_recv[hh, 1, rows(h), :].astype(jnp.float32),
                    )

                send_results(hh, 2, shard)
                return 0

            lax.fori_loop(0, RING, finish, 0)

        return 0

    lax.fori_loop(0, HEADS_EACH * RING, step, 0)

    def drain(k, _):
        target = member(k)
        for a in (2, 3):
            in_copy(1, a, target).wait_send()
        for hh in range(HEADS_EACH):
            for a in range(4):
                out_copy(hh, a, target).wait_send()
        return 0

    lax.fori_loop(1, RING, drain, 0)

    def drain_halo(h, _):
        for hh in range(HEADS_EACH):
            for a in range(2):
                fwd_copy(hh, a, h + RING - REACH).wait_send()
                back_copy(hh, a, h).wait_send()
        return 0

    lax.fori_loop(0, REACH, drain_halo, 0)

    def drain_results(source, _):
        for hh in range(HEADS_EACH):
            for a in range(4):
                landed(results[a].at[:, head_cols(source, hh)], out_recv.at[hh, a, source])
        return 0

    lax.fori_loop(0, RING, drain_results, 0)


def solution(mesh):
    n_blk = mesh.shape["blk"]

    def on_device(queries, key_rows, value_rows, out_grad, doc_lengths):
        tok, width = queries.shape
        group_rows, keys = RING * tok, (RING + REACH) * tok
        halo, window = REACH * tok, (REACH + 1) * tok
        low, full = jnp.bfloat16, jnp.float32
        dma = pltpu.SemaphoreType.DMA
        out = jax.ShapeDtypeStruct((tok, width), low)
        any_space = pl.BlockSpec(memory_space=pl.ANY)
        flops = 6 * 2 * HEADS_EACH * RING * tok * window * HEAD_DIM
        return pl.pallas_call(
            functools.partial(kernel, n_blk, tok),
            out_shape=[out] * 4,
            in_specs=[pl.BlockSpec(memory_space=pltpu.SMEM)] + [any_space] * 4,
            out_specs=[any_space] * 4,
            scratch_shapes=[
                pltpu.VMEM((HEADS_EACH, keys, HEAD_DIM), low),
                pltpu.VMEM((HEADS_EACH, keys, HEAD_DIM), low),
                pltpu.VMEM((HEADS_EACH, group_rows, HEAD_DIM), low),
                pltpu.VMEM((HEADS_EACH, group_rows, HEAD_DIM), low),
                pltpu.VMEM((HEAD_DIM, keys), low),
                pltpu.VMEM((HEAD_DIM, keys), low),
                pltpu.VMEM((RING, tok), jnp.int32),
                pltpu.VMEM((window, tok), full),
                pltpu.VMEM((window, tok), full),
                pltpu.VMEM((window, tok), low),
                pltpu.VMEM((window, tok), low),
                pltpu.VMEM((keys, HEAD_DIM), full),
                pltpu.VMEM((keys, HEAD_DIM), full),
                pltpu.VMEM((HEADS_EACH, 2, group_rows, HEAD_DIM), low),
                pltpu.VMEM((HEADS_EACH, 2, group_rows, HEAD_DIM), low),
                pltpu.VMEM((HEADS_EACH, 2, halo, HEAD_DIM), low),
                pltpu.VMEM((HEADS_EACH, 2, halo, HEAD_DIM), low),
                dma((HEADS_EACH, 4, RING)),
                dma((HEADS_EACH, 4, RING)),
                dma((HEADS_EACH, 2, REACH)),
                dma((HEADS_EACH, 2, REACH)),
                dma((HEADS_EACH, 2, REACH)),
                dma((HEADS_EACH, 2, REACH)),
                dma((HEADS_EACH, 4, RING)),
                dma((HEADS_EACH, 4, RING)),
            ],
            compiler_params=pltpu.CompilerParams(
                collective_id=0, has_side_effects=True, vmem_limit_bytes=56 * 2**20
            ),
            cost_estimate=pl.CostEstimate(
                flops=flops, bytes_accessed=16 * tok * width, transcendentals=0
            ),
        )(doc_lengths, queries, key_rows, value_rows, out_grad)

    rows_spec = P(("dp", "blk"), None)
    return jax.shard_map(
        on_device,
        mesh=mesh,
        in_specs=(rows_spec,) * 4 + (P("dp"),),
        out_specs=(rows_spec,) * 4,
        check_vma=False,
    )
```

```python
import functools
import math

import jax
import jax.numpy as jnp
from jax import lax
from jax.experimental import pallas as pl
from jax.experimental.pallas import tpu as pltpu
from jax.sharding import PartitionSpec as P

HEAD_DIM = 128
REACH = 6
RING = 8
HEADS_EACH = 2
PIECES = 2
NEG_FILL = -1e30
SCALE = 1.0 / math.sqrt(HEAD_DIM)
SCALE_LOG2 = SCALE * math.log2(math.e)
MESH = pl.DeviceIdType.MESH


def dot_nt(a, b):
    return lax.dot_general(a, b, (((1,), (1,)), ((), ())), preferred_element_type=jnp.float32)


def dot_nn(a, b):
    return jnp.dot(a, b, preferred_element_type=jnp.float32)


def kernel(
    n_blk, tok,
    doc_lengths, q_in, k_in, v_in, g_in,
    o_out, dq_out, dk_out, dv_out,
    k_buf, v_buf, q_buf, g_buf, kt, vt, start_ref,
    s_ref, d_ref, p_ref, ds_ref, acc_k, acc_v,
    o_stage, kv_stage, halo_send, halo_recv,
    in_send, in_recv, fwd_send, fwd_recv, back_send, back_recv, out_send, out_recv,
):
    me = lax.axis_index("blk")
    group, rank = me // RING, lax.rem(me, RING)
    n_groups = n_blk // RING
    window = (REACH + 1) * tok
    halo = REACH * tok

    def ring_device(member):
        return {"blk": group * RING + member}

    next_device = {"blk": lax.rem(group + 1, n_groups) * RING + rank}
    prev_device = {"blk": lax.rem(group + n_groups - 1, n_groups) * RING + rank}

    def member(k):
        return lax.rem(rank + k + RING, RING)

    def head_cols(owner, hh):
        return pl.ds(pl.multiple_of((owner * HEADS_EACH + hh) * HEAD_DIM, HEAD_DIM), HEAD_DIM)

    def rows(shard):
        return pl.ds(pl.multiple_of(shard * tok, tok), tok)

    def landed(ref, sem):
        pltpu.make_async_copy(ref, ref, sem).wait()

    sources = (k_in, v_in, q_in, g_in)

    def slot(hh, a, shard):
        if a < 2:
            return (k_buf, v_buf)[a].at[hh, rows(shard + REACH), :]
        return (q_buf, g_buf)[a - 2].at[hh, rows(shard), :]

    def in_copy(hh, a, target):
        return pltpu.make_async_remote_copy(
            src_ref=sources[a].at[:, head_cols(target, hh)],
            dst_ref=slot(hh, a, rank),
            send_sem=in_send.at[hh, a, target],
            recv_sem=in_recv.at[hh, a, rank],
            device_id=ring_device(target),
            device_id_type=MESH,
        )

    def own_copy(hh, a):
        return pltpu.make_async_copy(
            sources[a].at[:, head_cols(rank, hh)], slot(hh, a, rank), in_recv.at[hh, a, rank]
        )

    def in_landed(hh, a, shard):
        landed(slot(hh, a, shard), in_recv.at[hh, a, shard])

    def fwd_copy(hh, a, shard):
        h = shard - (RING - REACH)
        return pltpu.make_async_remote_copy(
            src_ref=slot(hh, a, shard),
            dst_ref=(k_buf, v_buf)[a].at[hh, rows(h), :],
            send_sem=fwd_send.at[hh, a, h],
            recv_sem=fwd_recv.at[hh, a, h],
            device_id=next_device,
            device_id_type=MESH,
        )

    def forward(hh, shard):
        for a in range(2):
            in_landed(hh, a, shard)

        @pl.when(shard >= RING - REACH)
        def _():
            for a in range(2):
                fwd_copy(hh, a, shard).start()

    def back_copy(hh, a, h):
        return pltpu.make_async_remote_copy(
            src_ref=halo_send.at[hh, a, rows(h), :],
            dst_ref=halo_recv.at[hh, a, rows(h), :],
            send_sem=back_send.at[hh, a, h],
            recv_sem=back_recv.at[hh, a, h],
            device_id=prev_device,
            device_id_type=MESH,
        )

    results = (o_out, dq_out, dk_out, dv_out)

    def staged(hh, a, shard):
        if a < 2:
            return o_stage.at[hh, a, rows(shard), :]
        return kv_stage.at[hh, a - 2, rows(shard), :]

    def out_copy(hh, a, target):
        return pltpu.make_async_remote_copy(
            src_ref=staged(hh, a, target),
            dst_ref=results[a].at[:, head_cols(rank, hh)],
            send_sem=out_send.at[hh, a, target],
            recv_sem=out_recv.at[hh, a, rank],
            device_id=ring_device(target),
            device_id_type=MESH,
        )

    def send_results(hh, first, target):
        @pl.when(target != rank)
        def _():
            for a in (first, first + 1):
                out_copy(hh, a, target).start()

        @pl.when(target == rank)
        def _():
            for a in (first, first + 1):
                pltpu.make_async_copy(
                    staged(hh, a, target),
                    results[a].at[:, head_cols(rank, hh)],
                    out_recv.at[hh, a, rank],
                ).start()

    barrier = pltpu.get_barrier_semaphore()
    for k in range(1, RING):
        pl.semaphore_signal(barrier, inc=1, device_id=ring_device(member(k)), device_id_type=MESH)
    pl.semaphore_signal(barrier, inc=1, device_id=next_device, device_id_type=MESH)
    pl.semaphore_signal(barrier, inc=1, device_id=prev_device, device_id_type=MESH)
    pl.semaphore_wait(barrier, RING + 1)

    def start_kv0(k, _):
        for a in (0, 1):
            in_copy(0, a, member(k)).start()
        return 0

    lax.fori_loop(1, RING, start_kv0, 0)
    for hh in range(HEADS_EACH):
        for a in range(4):
            own_copy(hh, a).start()

    position = group * RING * tok + (
        lax.broadcasted_iota(jnp.int32, (RING, tok), 0) * tok
        + lax.broadcasted_iota(jnp.int32, (RING, tok), 1)
    )
    first_key = jnp.zeros((RING, tok), jnp.int32)
    doc_end = jnp.int32(0)
    for j in range(doc_lengths.shape[0]):
        doc_end = doc_end + doc_lengths[j]
        first_key = jnp.where(position >= doc_end, doc_end, first_key)
    window_base = group * RING * tok - halo + lax.broadcasted_iota(jnp.int32, (RING, tok), 0) * tok
    start_ref[...] = first_key - window_base

    forward(0, rank)

    def start_qg0(k, _):
        target = member(k)
        for a in (0, 1):
            in_copy(0, a, target).wait_send()
        for a in (2, 3):
            in_copy(0, a, target).start()
        forward(0, member(-k))
        return 0

    lax.fori_loop(1, RING, start_qg0, 0)

    def start_kv1(k, _):
        target = member(k)
        for a in (2, 3):
            in_copy(0, a, target).wait_send()
        for a in (0, 1):
            in_copy(1, a, target).start()
        return 0

    lax.fori_loop(1, RING, start_kv1, 0)
    forward(1, rank)

    def transposed(hh, shard):
        kt[:, rows(shard)] = k_buf[hh, rows(shard), :].T
        vt[:, rows(shard)] = v_buf[hh, rows(shard), :].T

    key_row = lax.broadcasted_iota(jnp.int32, (tok, tok), 0)
    query_col = lax.broadcasted_iota(jnp.int32, (tok, tok), 1)

    def attend(hh, i):
        win = pl.ds(pl.multiple_of(i * tok, tok), window)
        q = q_buf[hh, rows(i), :]
        g = g_buf[hh, rows(i), :]
        start = start_ref[pl.ds(i, 1), :]
        s_ref[...] = dot_nt(k_buf[hh, win, :], q)
        top = None
        for b in range(REACH + 1):
            block = pl.ds(b * tok, tok)
            allowed = key_row >= start - b * tok
            if b == REACH:
                allowed = allowed & (key_row <= query_col)
            s = jnp.where(allowed, s_ref[block, :], NEG_FILL)
            s_ref[block, :] = s
            block_top = jnp.max(s, axis=0, keepdims=True)
            top = block_top if top is None else jnp.maximum(top, block_top)
        top = top * SCALE_LOG2
        total = None
        for b in range(REACH + 1):
            block = pl.ds(b * tok, tok)
            p = jnp.exp2(s_ref[block, :] * SCALE_LOG2 - top)
            s_ref[block, :] = p
            block_total = jnp.sum(p, axis=0, keepdims=True)
            total = block_total if total is None else total + block_total
        inverse = 1.0 / total
        for b in range(REACH + 1):
            block = pl.ds(b * tok, tok)
            p = s_ref[block, :] * inverse
            s_ref[block, :] = p
            p_ref[block, :] = p.astype(jnp.bfloat16)
        attended = dot_nn(vt[:, win], p_ref[...]).astype(jnp.bfloat16)
        o_stage[hh, 0, rows(i), :] = attended.T
        delta = jnp.sum(
            attended.astype(jnp.float32) * g.T.astype(jnp.float32), axis=0, keepdims=True
        )
        d_ref[...] = dot_nt(v_buf[hh, win, :], g)
        for b in range(REACH + 1):
            block = pl.ds(b * tok, tok)
            ds_ref[block, :] = (s_ref[block, :] * (d_ref[block, :] - delta)).astype(jnp.bfloat16)
        dq = dot_nn(kt[:, win], ds_ref[...]) * SCALE
        acc_k[win, :] += dot_nn(ds_ref[...], q)
        acc_v[win, :] += dot_nn(p_ref[...], g)
        o_stage[hh, 1, rows(i), :] = dq.astype(jnp.bfloat16).T

    def step(t, _):
        hh, i = t // RING, lax.rem(t, RING)

        @pl.when(i == 0)
        def _():
            acc_k[...] = jnp.zeros_like(acc_k)
            acc_v[...] = jnp.zeros_like(acc_v)

            def one(h, _):
                landed(k_buf.at[hh, rows(h), :], fwd_recv.at[hh, 0, h])
                landed(v_buf.at[hh, rows(h), :], fwd_recv.at[hh, 1, h])
                transposed(hh, h)
                return 0

            lax.fori_loop(0, REACH, one, 0)

        @pl.when((t >= 1) & (t < RING))
        def _():
            target = member(t)
            for a in (0, 1):
                in_copy(1, a, target).wait_send()
            for a in (2, 3):
                in_copy(1, a, target).start()
            forward(1, member(-t))

        for a in (2, 3):
            in_landed(hh, a, i)
        transposed(hh, i + REACH)
        attend(hh, i)
        send_results(hh, 0, i)

        @pl.when(i < REACH)
        def _():
            halo_send[hh, 0, rows(i), :] = (acc_k[rows(i), :] * SCALE).astype(jnp.bfloat16)
            halo_send[hh, 1, rows(i), :] = acc_v[rows(i), :].astype(jnp.bfloat16)
            for a in range(2):
                back_copy(hh, a, i).start()

        @pl.when(i == RING - 1)
        def _():
            def finish(k, _):
                shard = member(k)

                def put(dk, dv):
                    kv_stage[hh, 0, rows(shard), :] = dk.astype(jnp.bfloat16)
                    kv_stage[hh, 1, rows(shard), :] = dv.astype(jnp.bfloat16)

                own = rows(shard + REACH)

                @pl.when(shard < RING - REACH)
                def _():
                    put(acc_k[own, :] * SCALE, acc_v[own, :])

                @pl.when(shard >= RING - REACH)
                def _():
                    h = shard - (RING - REACH)
                    for a in range(2):
                        landed(halo_recv.at[hh, a, rows(h), :], back_recv.at[hh, a, h])
                    put(
                        acc_k[own, :] * SCALE + halo_recv[hh, 0, rows(h), :].astype(jnp.float32),
                        acc_v[own, :] + halo_recv[hh, 1, rows(h), :].astype(jnp.float32),
                    )

                send_results(hh, 2, shard)
                return 0

            lax.fori_loop(0, RING, finish, 0)

        return 0

    lax.fori_loop(0, HEADS_EACH * RING, step, 0)

    def drain(k, _):
        target = member(k)
        for a in (2, 3):
            in_copy(1, a, target).wait_send()
        for hh in range(HEADS_EACH):
            for a in range(4):
                out_copy(hh, a, target).wait_send()
        return 0

    lax.fori_loop(1, RING, drain, 0)

    def drain_halo(h, _):
        for hh in range(HEADS_EACH):
            for a in range(2):
                fwd_copy(hh, a, h + RING - REACH).wait_send()
                back_copy(hh, a, h).wait_send()
        return 0

    lax.fori_loop(0, REACH, drain_halo, 0)

    def drain_results(source, _):
        for hh in range(HEADS_EACH):
            for a in range(4):
                landed(results[a].at[:, head_cols(source, hh)], out_recv.at[hh, a, source])
        return 0

    lax.fori_loop(0, RING, drain_results, 0)


def write_out(*refs):
    sources, targets, sems = refs[:4], refs[4:8], refs[8]
    part = sources[0].shape[0] // PIECES
    copies = [
        pltpu.make_async_copy(
            sources[a].at[pl.ds(n * part, part), :],
            targets[a].at[pl.ds(n * part, part), :],
            sems.at[a, n],
        )
        for n in range(PIECES)
        for a in range(4)
    ]
    for copy in copies:
        copy.start()
    for copy in copies:
        copy.wait()


def solution(mesh):
    n_blk = mesh.shape["blk"]

    def on_device(queries, key_rows, value_rows, out_grad, doc_lengths):
        tok, width = queries.shape
        group_rows, keys = RING * tok, (RING + REACH) * tok
        halo, window = REACH * tok, (REACH + 1) * tok
        low, full = jnp.bfloat16, jnp.float32
        dma = pltpu.SemaphoreType.DMA
        landing = pltpu.VMEM((tok, width), low)
        out = jax.ShapeDtypeStruct((tok, width), low)
        any_space = pl.BlockSpec(memory_space=pl.ANY)
        flops = 6 * 2 * HEADS_EACH * RING * tok * window * HEAD_DIM
        results = pl.pallas_call(
            functools.partial(kernel, n_blk, tok),
            out_shape=[landing] * 4,
            in_specs=[pl.BlockSpec(memory_space=pltpu.SMEM)] + [any_space] * 4,
            out_specs=[any_space] * 4,
            scratch_shapes=[
                pltpu.VMEM((HEADS_EACH, keys, HEAD_DIM), low),
                pltpu.VMEM((HEADS_EACH, keys, HEAD_DIM), low),
                pltpu.VMEM((HEADS_EACH, group_rows, HEAD_DIM), low),
                pltpu.VMEM((HEADS_EACH, group_rows, HEAD_DIM), low),
                pltpu.VMEM((HEAD_DIM, keys), low),
                pltpu.VMEM((HEAD_DIM, keys), low),
                pltpu.VMEM((RING, tok), jnp.int32),
                pltpu.VMEM((window, tok), full),
                pltpu.VMEM((window, tok), full),
                pltpu.VMEM((window, tok), low),
                pltpu.VMEM((window, tok), low),
                pltpu.VMEM((keys, HEAD_DIM), full),
                pltpu.VMEM((keys, HEAD_DIM), full),
                pltpu.VMEM((HEADS_EACH, 2, group_rows, HEAD_DIM), low),
                pltpu.VMEM((HEADS_EACH, 2, group_rows, HEAD_DIM), low),
                pltpu.VMEM((HEADS_EACH, 2, halo, HEAD_DIM), low),
                pltpu.VMEM((HEADS_EACH, 2, halo, HEAD_DIM), low),
                dma((HEADS_EACH, 4, RING)),
                dma((HEADS_EACH, 4, RING)),
                dma((HEADS_EACH, 2, REACH)),
                dma((HEADS_EACH, 2, REACH)),
                dma((HEADS_EACH, 2, REACH)),
                dma((HEADS_EACH, 2, REACH)),
                dma((HEADS_EACH, 4, RING)),
                dma((HEADS_EACH, 4, RING)),
            ],
            compiler_params=pltpu.CompilerParams(
                collective_id=0, has_side_effects=True, vmem_limit_bytes=58 * 2**20
            ),
            cost_estimate=pl.CostEstimate(
                flops=flops, bytes_accessed=16 * tok * width, transcendentals=0
            ),
        )(doc_lengths, queries, key_rows, value_rows, out_grad)
        return pl.pallas_call(
            write_out,
            out_shape=[out] * 4,
            in_specs=[any_space] * 4,
            out_specs=[any_space] * 4,
            scratch_shapes=[dma((4, PIECES))],
            compiler_params=pltpu.CompilerParams(vmem_limit_bytes=2**20),
            cost_estimate=pl.CostEstimate(
                flops=0, bytes_accessed=16 * tok * width, transcendentals=0
            ),
        )(*[pltpu.with_memory_space_constraint(r, pltpu.VMEM) for r in results])

    rows_spec = P(("dp", "blk"), None)
    return jax.shard_map(
        on_device,
        mesh=mesh,
        in_specs=(rows_spec,) * 4 + (P("dp"),),
        out_specs=(rows_spec,) * 4,
        check_vma=False,
    )
```

```python
import functools
import math

import jax
import jax.numpy as jnp
from jax import lax
from jax.experimental import pallas as pl
from jax.experimental.pallas import tpu as pltpu
from jax.sharding import PartitionSpec as P

HEAD_DIM = 128
REACH = 6
RING = 8
HEADS_EACH = 2
PIECES = 1
WINDOW = 12
NEG_FILL = -1e30
SCALE = 1.0 / math.sqrt(HEAD_DIM)
SCALE_LOG2 = SCALE * math.log2(math.e)
MESH = pl.DeviceIdType.MESH


def dot_nt(a, b):
    return lax.dot_general(a, b, (((1,), (1,)), ((), ())), preferred_element_type=jnp.float32)


def dot_nn(a, b):
    return jnp.dot(a, b, preferred_element_type=jnp.float32)


def kernel(
    n_blk, tok,
    doc_lengths, q_in, k_in, v_in, g_in,
    o_out, dq_out, dk_out, dv_out,
    k_buf, v_buf, q_buf, g_buf, kt, vt, start_ref,
    s_ref, d_ref, p_ref, ds_ref, acc_k, acc_v,
    o_stage, kv_stage, halo_send, halo_recv,
    in_send, in_recv, fwd_send, fwd_recv, back_send, back_recv, out_send, out_recv,
):
    me = lax.axis_index("blk")
    group, rank = me // RING, lax.rem(me, RING)
    n_groups = n_blk // RING
    window = (REACH + 1) * tok
    halo = REACH * tok

    def ring_device(member):
        return {"blk": group * RING + member}

    has_prev, has_next = group > 0, group < n_groups - 1
    next_device = {"blk": lax.rem(group + 1, n_groups) * RING + rank}
    prev_device = {"blk": lax.rem(group + n_groups - 1, n_groups) * RING + rank}

    def member(k):
        return lax.rem(rank + k + RING, RING)

    def head_cols(owner, hh):
        return pl.ds(pl.multiple_of((owner * HEADS_EACH + hh) * HEAD_DIM, HEAD_DIM), HEAD_DIM)

    def rows(shard):
        return pl.ds(pl.multiple_of(shard * tok, tok), tok)

    def landed(ref, sem):
        pltpu.make_async_copy(ref, ref, sem).wait()

    sources = (k_in, v_in, q_in, g_in)

    def slot(hh, a, shard):
        if a < 2:
            return (k_buf, v_buf)[a].at[hh, rows(shard + REACH), :]
        return (q_buf, g_buf)[a - 2].at[hh, rows(shard), :]

    def in_copy(hh, a, target):
        return pltpu.make_async_remote_copy(
            src_ref=sources[a].at[:, head_cols(target, hh)],
            dst_ref=slot(hh, a, rank),
            send_sem=in_send.at[hh, a, target],
            recv_sem=in_recv.at[hh, a, rank],
            device_id=ring_device(target),
            device_id_type=MESH,
        )

    def own_copy(hh, a):
        return pltpu.make_async_copy(
            sources[a].at[:, head_cols(rank, hh)], slot(hh, a, rank), in_recv.at[hh, a, rank]
        )

    def in_landed(hh, a, shard):
        landed(slot(hh, a, shard), in_recv.at[hh, a, shard])

    def fwd_copy(hh, a, shard):
        h = shard - (RING - REACH)
        return pltpu.make_async_remote_copy(
            src_ref=slot(hh, a, shard),
            dst_ref=(k_buf, v_buf)[a].at[hh, rows(h), :],
            send_sem=fwd_send.at[hh, a, h],
            recv_sem=fwd_recv.at[hh, a, h],
            device_id=next_device,
            device_id_type=MESH,
        )

    def forward(hh, shard):
        for a in range(2):
            in_landed(hh, a, shard)

        @pl.when((shard >= RING - REACH) & has_next)
        def _():
            for a in range(2):
                fwd_copy(hh, a, shard).start()

    def back_copy(hh, a, h):
        return pltpu.make_async_remote_copy(
            src_ref=halo_send.at[hh, a, rows(h), :],
            dst_ref=halo_recv.at[hh, a, rows(h), :],
            send_sem=back_send.at[hh, a, h],
            recv_sem=back_recv.at[hh, a, h],
            device_id=prev_device,
            device_id_type=MESH,
        )

    results = (o_out, dq_out, dk_out, dv_out)

    def staged(hh, a, shard):
        if a < 2:
            return o_stage.at[hh, a, rows(shard), :]
        return kv_stage.at[hh, a - 2, rows(shard), :]

    def out_copy(hh, a, target):
        return pltpu.make_async_remote_copy(
            src_ref=staged(hh, a, target),
            dst_ref=results[a].at[:, head_cols(rank, hh)],
            send_sem=out_send.at[a],
            recv_sem=out_recv.at[a],
            device_id=ring_device(target),
            device_id_type=MESH,
        )

    def send_results(hh, first, target):
        @pl.when(target != rank)
        def _():
            for a in (first, first + 1):
                out_copy(hh, a, target).start()

        @pl.when(target == rank)
        def _():
            for a in (first, first + 1):
                pltpu.make_async_copy(
                    staged(hh, a, target),
                    results[a].at[:, head_cols(rank, hh)],
                    out_recv.at[a],
                ).start()

    barrier = pltpu.get_barrier_semaphore()
    for k in range(1, RING):
        pl.semaphore_signal(barrier, inc=1, device_id=ring_device(member(k)), device_id_type=MESH)

    @pl.when(has_next)
    def _():
        pl.semaphore_signal(barrier, inc=1, device_id=next_device, device_id_type=MESH)

    @pl.when(has_prev)
    def _():
        pl.semaphore_signal(barrier, inc=1, device_id=prev_device, device_id_type=MESH)

    pl.semaphore_wait(barrier, RING - 1 + has_next.astype(jnp.int32) + has_prev.astype(jnp.int32))

    sends = [(hh, a, k) for hh in range(HEADS_EACH) for a in (0, 2) for k in range(1, RING)]
    paced = (2 * HEADS_EACH - 1) * (RING - 1)

    def start_send(n):
        hh, a, k = sends[n]
        for b in (a, a + 1):
            in_copy(hh, b, member(k)).start()

    def wait_send(n):
        hh, a, k = sends[n]
        for b in (a, a + 1):
            in_copy(hh, b, member(k)).wait_send()

    for n in range(WINDOW):
        start_send(n)
    for hh in range(HEADS_EACH):
        for a in range(4):
            own_copy(hh, a).start()

    @pl.when(jnp.logical_not(has_prev))
    def _():
        for buf in (k_buf, v_buf):
            buf[:, :halo, :] = jnp.zeros((HEADS_EACH, halo, HEAD_DIM), buf.dtype)

    @pl.when(jnp.logical_not(has_next))
    def _():
        halo_recv[...] = jnp.zeros_like(halo_recv)

    position = group * RING * tok + (
        lax.broadcasted_iota(jnp.int32, (RING, tok), 0) * tok
        + lax.broadcasted_iota(jnp.int32, (RING, tok), 1)
    )
    first_key = jnp.zeros((RING, tok), jnp.int32)
    doc_end = jnp.int32(0)
    for j in range(doc_lengths.shape[0]):
        doc_end = doc_end + doc_lengths[j]
        first_key = jnp.where(position >= doc_end, doc_end, first_key)
    window_base = group * RING * tok - halo + lax.broadcasted_iota(jnp.int32, (RING, tok), 0) * tok
    start_ref[...] = first_key - window_base

    forward(0, rank)

    for n in range(WINDOW, paced):
        wait_send(n - WINDOW)
        start_send(n)
        if n - WINDOW < RING - 1:
            forward(0, member(-(n - WINDOW + 1)))
    forward(1, rank)

    def transposed(hh, shard):
        kt[:, rows(shard)] = k_buf[hh, rows(shard), :].T
        vt[:, rows(shard)] = v_buf[hh, rows(shard), :].T

    key_row = lax.broadcasted_iota(jnp.int32, (tok, tok), 0)
    query_col = lax.broadcasted_iota(jnp.int32, (tok, tok), 1)

    def attend(hh, i):
        win = pl.ds(pl.multiple_of(i * tok, tok), window)
        q = q_buf[hh, rows(i), :]
        g = g_buf[hh, rows(i), :]
        start = start_ref[pl.ds(i, 1), :]
        s_ref[...] = dot_nt(k_buf[hh, win, :], q)
        top = None
        for b in range(REACH + 1):
            block = pl.ds(b * tok, tok)
            allowed = key_row >= start - b * tok
            if b == REACH:
                allowed = allowed & (key_row <= query_col)
            s = jnp.where(allowed, s_ref[block, :], NEG_FILL)
            s_ref[block, :] = s
            block_top = jnp.max(s, axis=0, keepdims=True)
            top = block_top if top is None else jnp.maximum(top, block_top)
        top = top * SCALE_LOG2
        total = None
        for b in range(REACH + 1):
            block = pl.ds(b * tok, tok)
            p = jnp.exp2(s_ref[block, :] * SCALE_LOG2 - top)
            s_ref[block, :] = p
            block_total = jnp.sum(p, axis=0, keepdims=True)
            total = block_total if total is None else total + block_total
        inverse = 1.0 / total
        for b in range(REACH + 1):
            block = pl.ds(b * tok, tok)
            p = s_ref[block, :] * inverse
            s_ref[block, :] = p
            p_ref[block, :] = p.astype(jnp.bfloat16)
        attended = dot_nn(vt[:, win], p_ref[...]).astype(jnp.bfloat16)
        o_stage[hh, 0, rows(i), :] = attended.T
        delta = jnp.sum(
            attended.astype(jnp.float32) * g.T.astype(jnp.float32), axis=0, keepdims=True
        )
        d_ref[...] = dot_nt(v_buf[hh, win, :], g)
        for b in range(REACH + 1):
            block = pl.ds(b * tok, tok)
            ds_ref[block, :] = (s_ref[block, :] * (d_ref[block, :] - delta)).astype(jnp.bfloat16)
        dq = dot_nn(kt[:, win], ds_ref[...]) * SCALE
        acc_k[win, :] += dot_nn(ds_ref[...], q)
        acc_v[win, :] += dot_nn(p_ref[...], g)
        o_stage[hh, 1, rows(i), :] = dq.astype(jnp.bfloat16).T

    def step(t, _):
        hh, i = t // RING, lax.rem(t, RING)

        @pl.when(i == 0)
        def _():
            acc_k[...] = jnp.zeros_like(acc_k)
            acc_v[...] = jnp.zeros_like(acc_v)

            def one(h, _):
                @pl.when(has_prev)
                def _():
                    landed(k_buf.at[hh, rows(h), :], fwd_recv.at[hh, 0, h])
                    landed(v_buf.at[hh, rows(h), :], fwd_recv.at[hh, 1, h])

                transposed(hh, h)
                return 0

            lax.fori_loop(0, REACH, one, 0)

        @pl.when(t * 2 < RING - 1)
        def _():
            for n in range(2):
                k = t * 2 + n + 1

                @pl.when(k < RING)
                def _():
                    for a in (2, 3):
                        in_copy(1, a, member(k)).start()

        @pl.when((t >= 1) & (t < RING))
        def _():
            forward(1, member(-t))

        for a in (2, 3):
            in_landed(hh, a, i)
        transposed(hh, i + REACH)
        attend(hh, i)
        send_results(hh, 0, i)

        @pl.when((i < REACH) & has_prev)
        def _():
            halo_send[hh, 0, rows(i), :] = (acc_k[rows(i), :] * SCALE).astype(jnp.bfloat16)
            halo_send[hh, 1, rows(i), :] = acc_v[rows(i), :].astype(jnp.bfloat16)
            for a in range(2):
                back_copy(hh, a, i).start()

        @pl.when(i == RING - 1)
        def _():
            def finish(k, _):
                shard = member(k)

                def put(dk, dv):
                    kv_stage[hh, 0, rows(shard), :] = dk.astype(jnp.bfloat16)
                    kv_stage[hh, 1, rows(shard), :] = dv.astype(jnp.bfloat16)

                own = rows(shard + REACH)

                @pl.when(shard < RING - REACH)
                def _():
                    put(acc_k[own, :] * SCALE, acc_v[own, :])

                @pl.when(shard >= RING - REACH)
                def _():
                    h = shard - (RING - REACH)

                    @pl.when(has_next)
                    def _():
                        for a in range(2):
                            landed(halo_recv.at[hh, a, rows(h), :], back_recv.at[hh, a, h])

                    put(
                        acc_k[own, :] * SCALE + halo_recv[hh, 0, rows(h), :].astype(jnp.float32),
                        acc_v[own, :] + halo_recv[hh, 1, rows(h), :].astype(jnp.float32),
                    )

                send_results(hh, 2, shard)
                return 0

            lax.fori_loop(0, RING, finish, 0)

        return 0

    lax.fori_loop(0, HEADS_EACH * RING, step, 0)

    for n in range(paced - WINDOW, len(sends)):
        wait_send(n)
    def drain_halo(h, _):
        for hh in range(HEADS_EACH):
            for a in range(2):
                @pl.when(has_next)
                def _():
                    fwd_copy(hh, a, h + RING - REACH).wait_send()

                @pl.when(has_prev)
                def _():
                    back_copy(hh, a, h).wait_send()

        return 0

    lax.fori_loop(0, REACH, drain_halo, 0)

    for a in range(4):
        landed(k_buf.at[0], out_send.at[a])
        landed(results[a], out_recv.at[a])


def write_out(*refs):
    sources, targets, sems = refs[:4], refs[4:8], refs[8]
    part = sources[0].shape[0] // PIECES
    copies = [
        pltpu.make_async_copy(
            sources[a].at[pl.ds(n * part, part), :],
            targets[a].at[pl.ds(n * part, part), :],
            sems.at[a, n],
        )
        for n in range(PIECES)
        for a in range(4)
    ]
    for copy in copies:
        copy.start()
    for copy in copies:
        copy.wait()


def solution(mesh):
    n_blk = mesh.shape["blk"]

    def on_device(queries, key_rows, value_rows, out_grad, doc_lengths):
        tok, width = queries.shape
        group_rows, keys = RING * tok, (RING + REACH) * tok
        halo, window = REACH * tok, (REACH + 1) * tok
        low, full = jnp.bfloat16, jnp.float32
        dma = pltpu.SemaphoreType.DMA
        landing = pltpu.VMEM((tok, width), low)
        out = jax.ShapeDtypeStruct((tok, width), low)
        any_space = pl.BlockSpec(memory_space=pl.ANY)
        flops = 6 * 2 * HEADS_EACH * RING * tok * window * HEAD_DIM
        results = pl.pallas_call(
            functools.partial(kernel, n_blk, tok),
            out_shape=[landing] * 4,
            in_specs=[pl.BlockSpec(memory_space=pltpu.SMEM)] + [any_space] * 4,
            out_specs=[any_space] * 4,
            scratch_shapes=[
                pltpu.VMEM((HEADS_EACH, keys, HEAD_DIM), low),
                pltpu.VMEM((HEADS_EACH, keys, HEAD_DIM), low),
                pltpu.VMEM((HEADS_EACH, group_rows, HEAD_DIM), low),
                pltpu.VMEM((HEADS_EACH, group_rows, HEAD_DIM), low),
                pltpu.VMEM((HEAD_DIM, keys), low),
                pltpu.VMEM((HEAD_DIM, keys), low),
                pltpu.VMEM((RING, tok), jnp.int32),
                pltpu.VMEM((window, tok), full),
                pltpu.VMEM((window, tok), full),
                pltpu.VMEM((window, tok), low),
                pltpu.VMEM((window, tok), low),
                pltpu.VMEM((keys, HEAD_DIM), full),
                pltpu.VMEM((keys, HEAD_DIM), full),
                pltpu.VMEM((HEADS_EACH, 2, group_rows, HEAD_DIM), low),
                pltpu.VMEM((HEADS_EACH, 2, group_rows, HEAD_DIM), low),
                pltpu.VMEM((HEADS_EACH, 2, halo, HEAD_DIM), low),
                pltpu.VMEM((HEADS_EACH, 2, halo, HEAD_DIM), low),
                dma((HEADS_EACH, 4, RING)),
                dma((HEADS_EACH, 4, RING)),
                dma((HEADS_EACH, 2, REACH)),
                dma((HEADS_EACH, 2, REACH)),
                dma((HEADS_EACH, 2, REACH)),
                dma((HEADS_EACH, 2, REACH)),
                dma((4,)),
                dma((4,)),
            ],
            compiler_params=pltpu.CompilerParams(
                collective_id=0, has_side_effects=True, vmem_limit_bytes=58 * 2**20
            ),
            cost_estimate=pl.CostEstimate(
                flops=flops, bytes_accessed=16 * tok * width, transcendentals=0
            ),
        )(doc_lengths, queries, key_rows, value_rows, out_grad)
        return pl.pallas_call(
            write_out,
            out_shape=[out] * 4,
            in_specs=[any_space] * 4,
            out_specs=[any_space] * 4,
            scratch_shapes=[dma((4, PIECES))],
            compiler_params=pltpu.CompilerParams(vmem_limit_bytes=2**20),
            cost_estimate=pl.CostEstimate(
                flops=0, bytes_accessed=16 * tok * width, transcendentals=0
            ),
        )(*[pltpu.with_memory_space_constraint(r, pltpu.VMEM) for r in results])

    rows_spec = P(("dp", "blk"), None)
    return jax.shard_map(
        on_device,
        mesh=mesh,
        in_specs=(rows_spec,) * 4 + (P("dp"),),
        out_specs=(rows_spec,) * 4,
        check_vma=False,
    )
```

```python
import functools
import math

import jax
import jax.numpy as jnp
from jax import lax
from jax.experimental import pallas as pl
from jax.experimental.pallas import tpu as pltpu
from jax.sharding import PartitionSpec as P

HEAD_DIM = 128
REACH = 6
RING = 8
HEADS_EACH = 2
WINDOW = 12
NEG_FILL = -1e30
SCALE = 1.0 / math.sqrt(HEAD_DIM)
SCALE_LOG2 = SCALE * math.log2(math.e)
MESH = pl.DeviceIdType.MESH


def dot_nt(a, b):
    return lax.dot_general(a, b, (((1,), (1,)), ((), ())), preferred_element_type=jnp.float32)


def dot_nn(a, b):
    return jnp.dot(a, b, preferred_element_type=jnp.float32)


def kernel(
    n_blk, tok,
    doc_lengths_in, q_in, k_in, v_in, g_in,
    results,
    k_buf, v_buf, q_buf, g_buf, kt, vt, start_ref,
    s_ref, d_ref, p_ref, ds_ref, acc_k, acc_v,
    stage, halo_send, halo_recv,
    in_send, in_recv, fwd_send, fwd_recv, back_send, back_recv, out_send, out_recv,
    doc_lengths, doc_sem,
):
    me = lax.axis_index("blk")
    group, rank = me // RING, lax.rem(me, RING)
    n_groups = n_blk // RING
    window = (REACH + 1) * tok
    halo = REACH * tok

    def ring_device(member):
        return {"blk": group * RING + member}

    has_prev, has_next = group > 0, group < n_groups - 1
    next_device = {"blk": lax.rem(group + 1, n_groups) * RING + rank}
    prev_device = {"blk": lax.rem(group + n_groups - 1, n_groups) * RING + rank}

    def member(k):
        return lax.rem(rank + k + RING, RING)

    def head_cols(owner, hh):
        return pl.ds(pl.multiple_of((owner * HEADS_EACH + hh) * HEAD_DIM, HEAD_DIM), HEAD_DIM)

    def rows(shard):
        return pl.ds(pl.multiple_of(shard * tok, tok), tok)

    def landed(ref, sem):
        pltpu.make_async_copy(ref, ref, sem).wait()

    sources = (k_in, v_in, q_in, g_in)

    def slot(hh, a, shard):
        if a < 2:
            return (k_buf, v_buf)[a].at[hh, rows(shard + REACH), :]
        return (q_buf, g_buf)[a - 2].at[hh, rows(shard), :]

    def in_copy(hh, a, target):
        return pltpu.make_async_remote_copy(
            src_ref=sources[a].at[:, head_cols(target, hh)],
            dst_ref=slot(hh, a, rank),
            send_sem=in_send.at[hh, a, target],
            recv_sem=in_recv.at[hh, a, rank],
            device_id=ring_device(target),
            device_id_type=MESH,
        )

    def own_copy(hh, a):
        return pltpu.make_async_copy(
            sources[a].at[:, head_cols(rank, hh)], slot(hh, a, rank), in_recv.at[hh, a, rank]
        )

    def in_landed(hh, a, shard):
        landed(slot(hh, a, shard), in_recv.at[hh, a, shard])

    def fwd_copy(hh, a, shard):
        h = shard - (RING - REACH)
        return pltpu.make_async_remote_copy(
            src_ref=slot(hh, a, shard),
            dst_ref=(k_buf, v_buf)[a].at[hh, rows(h), :],
            send_sem=fwd_send.at[hh, a, h],
            recv_sem=fwd_recv.at[hh, a, h],
            device_id=next_device,
            device_id_type=MESH,
        )

    def forward(hh, shard):
        for a in range(2):
            in_landed(hh, a, shard)

        @pl.when((shard >= RING - REACH) & has_next)
        def _():
            for a in range(2):
                fwd_copy(hh, a, shard).start()

    def back_copy(hh, a, h):
        return pltpu.make_async_remote_copy(
            src_ref=halo_send.at[hh, a, rows(h), :],
            dst_ref=halo_recv.at[hh, a, rows(h), :],
            send_sem=back_send.at[hh, a, h],
            recv_sem=back_recv.at[hh, a, h],
            device_id=prev_device,
            device_id_type=MESH,
        )

    def out_pair(hh, first, target):
        pair = pl.ds(first, 2)
        return stage.at[hh, pair, rows(target), :], results.at[pair, :, head_cols(rank, hh)]

    def send_results(hh, first, target):
        source, landing = out_pair(hh, first, target)

        @pl.when(target != rank)
        def _():
            pltpu.make_async_remote_copy(
                src_ref=source,
                dst_ref=landing,
                send_sem=out_send.at[first // 2],
                recv_sem=out_recv.at[first // 2],
                device_id=ring_device(target),
                device_id_type=MESH,
            ).start()

        @pl.when(target == rank)
        def _():
            pltpu.make_async_copy(source, landing, out_recv.at[first // 2]).start()

    barrier = pltpu.get_barrier_semaphore()
    for k in range(1, RING):
        pl.semaphore_signal(barrier, inc=1, device_id=ring_device(member(k)), device_id_type=MESH)

    @pl.when(has_next)
    def _():
        pl.semaphore_signal(barrier, inc=1, device_id=next_device, device_id_type=MESH)

    @pl.when(has_prev)
    def _():
        pl.semaphore_signal(barrier, inc=1, device_id=prev_device, device_id_type=MESH)

    doc_copy = pltpu.make_async_copy(doc_lengths_in, doc_lengths, doc_sem)
    doc_copy.start()
    pl.semaphore_wait(barrier, RING - 1 + has_next.astype(jnp.int32) + has_prev.astype(jnp.int32))

    sends = [(hh, a, k) for hh in range(HEADS_EACH) for a in (0, 2) for k in range(1, RING)]
    paced = (2 * HEADS_EACH - 1) * (RING - 1)

    def start_send(n):
        hh, a, k = sends[n]
        for b in (a, a + 1):
            in_copy(hh, b, member(k)).start()

    def wait_send(n):
        hh, a, k = sends[n]
        for b in (a, a + 1):
            in_copy(hh, b, member(k)).wait_send()

    for n in range(WINDOW):
        start_send(n)
    for hh in range(HEADS_EACH):
        for a in range(4):
            own_copy(hh, a).start()

    @pl.when(jnp.logical_not(has_prev))
    def _():
        for buf in (k_buf, v_buf):
            buf[:, :halo, :] = jnp.zeros((HEADS_EACH, halo, HEAD_DIM), buf.dtype)

    @pl.when(jnp.logical_not(has_next))
    def _():
        halo_recv[...] = jnp.zeros_like(halo_recv)

    position = group * RING * tok + (
        lax.broadcasted_iota(jnp.int32, (RING, tok), 0) * tok
        + lax.broadcasted_iota(jnp.int32, (RING, tok), 1)
    )
    doc_copy.wait()
    first_key = jnp.zeros((RING, tok), jnp.int32)
    doc_end = jnp.int32(0)
    for j in range(doc_lengths.shape[0]):
        doc_end = doc_end + doc_lengths[j]
        first_key = jnp.where(position >= doc_end, doc_end, first_key)
    window_base = group * RING * tok - halo + lax.broadcasted_iota(jnp.int32, (RING, tok), 0) * tok
    start_ref[...] = first_key - window_base

    forward(0, rank)

    for n in range(WINDOW, paced):
        wait_send(n - WINDOW)
        start_send(n)
        if n - WINDOW < RING - 1:
            forward(0, member(-(n - WINDOW + 1)))
    forward(1, rank)

    def transposed(hh, shard):
        kt[:, rows(shard)] = k_buf[hh, rows(shard), :].T
        vt[:, rows(shard)] = v_buf[hh, rows(shard), :].T

    key_row = lax.broadcasted_iota(jnp.int32, (tok, tok), 0)
    query_col = lax.broadcasted_iota(jnp.int32, (tok, tok), 1)

    def attend(hh, i):
        win = pl.ds(pl.multiple_of(i * tok, tok), window)
        q = q_buf[hh, rows(i), :]
        g = g_buf[hh, rows(i), :]
        start = start_ref[pl.ds(i, 1), :]
        s_ref[...] = dot_nt(k_buf[hh, win, :], q)
        top = None
        for b in range(REACH + 1):
            block = pl.ds(b * tok, tok)
            allowed = key_row >= start - b * tok
            if b == REACH:
                allowed = allowed & (key_row <= query_col)
            s = jnp.where(allowed, s_ref[block, :], NEG_FILL)
            s_ref[block, :] = s
            block_top = jnp.max(s, axis=0, keepdims=True)
            top = block_top if top is None else jnp.maximum(top, block_top)
        top = top * SCALE_LOG2
        total = None
        for b in range(REACH + 1):
            block = pl.ds(b * tok, tok)
            p = jnp.exp2(s_ref[block, :] * SCALE_LOG2 - top)
            s_ref[block, :] = p
            block_total = jnp.sum(p, axis=0, keepdims=True)
            total = block_total if total is None else total + block_total
        inverse = 1.0 / total
        for b in range(REACH + 1):
            block = pl.ds(b * tok, tok)
            p = s_ref[block, :] * inverse
            s_ref[block, :] = p
            p_ref[block, :] = p.astype(jnp.bfloat16)
        attended = dot_nn(vt[:, win], p_ref[...]).astype(jnp.bfloat16)
        stage[hh, 0, rows(i), :] = attended.T
        delta = jnp.sum(
            attended.astype(jnp.float32) * g.T.astype(jnp.float32), axis=0, keepdims=True
        )
        d_ref[...] = dot_nt(v_buf[hh, win, :], g)
        for b in range(REACH + 1):
            block = pl.ds(b * tok, tok)
            ds_ref[block, :] = (s_ref[block, :] * (d_ref[block, :] - delta)).astype(jnp.bfloat16)
        dq = dot_nn(kt[:, win], ds_ref[...]) * SCALE
        acc_k[win, :] += dot_nn(ds_ref[...], q)
        acc_v[win, :] += dot_nn(p_ref[...], g)
        stage[hh, 1, rows(i), :] = dq.astype(jnp.bfloat16).T

    def step(t, _):
        hh, i = t // RING, lax.rem(t, RING)

        @pl.when(i == 0)
        def _():
            acc_k[...] = jnp.zeros_like(acc_k)
            acc_v[...] = jnp.zeros_like(acc_v)

            def one(h, _):
                @pl.when(has_prev)
                def _():
                    landed(k_buf.at[hh, rows(h), :], fwd_recv.at[hh, 0, h])
                    landed(v_buf.at[hh, rows(h), :], fwd_recv.at[hh, 1, h])

                transposed(hh, h)
                return 0

            lax.fori_loop(0, REACH, one, 0)

        @pl.when(t * 2 < RING - 1)
        def _():
            for n in range(2):
                k = t * 2 + n + 1

                @pl.when(k < RING)
                def _():
                    for a in (2, 3):
                        in_copy(1, a, member(k)).start()

        @pl.when((t >= 1) & (t < RING))
        def _():
            forward(1, member(-t))

        for a in (2, 3):
            in_landed(hh, a, i)
        transposed(hh, i + REACH)
        attend(hh, i)
        send_results(hh, 0, i)

        @pl.when((i < REACH) & has_prev)
        def _():
            halo_send[hh, 0, rows(i), :] = (acc_k[rows(i), :] * SCALE).astype(jnp.bfloat16)
            halo_send[hh, 1, rows(i), :] = acc_v[rows(i), :].astype(jnp.bfloat16)
            for a in range(2):
                back_copy(hh, a, i).start()

        @pl.when(i == RING - 1)
        def _():
            def finish(k, _):
                shard = member(k)

                def put(dk, dv):
                    stage[hh, 2, rows(shard), :] = dk.astype(jnp.bfloat16)
                    stage[hh, 3, rows(shard), :] = dv.astype(jnp.bfloat16)

                own = rows(shard + REACH)

                @pl.when(shard < RING - REACH)
                def _():
                    put(acc_k[own, :] * SCALE, acc_v[own, :])

                @pl.when(shard >= RING - REACH)
                def _():
                    h = shard - (RING - REACH)

                    @pl.when(has_next)
                    def _():
                        for a in range(2):
                            landed(halo_recv.at[hh, a, rows(h), :], back_recv.at[hh, a, h])

                    put(
                        acc_k[own, :] * SCALE + halo_recv[hh, 0, rows(h), :].astype(jnp.float32),
                        acc_v[own, :] + halo_recv[hh, 1, rows(h), :].astype(jnp.float32),
                    )

                send_results(hh, 2, shard)
                return 0

            lax.fori_loop(0, RING, finish, 0)

        return 0

    lax.fori_loop(0, HEADS_EACH * RING, step, 0)

    for n in range(paced - WINDOW, len(sends)):
        wait_send(n)
    def drain_halo(h, _):
        for hh in range(HEADS_EACH):
            for a in range(2):
                @pl.when(has_next)
                def _():
                    fwd_copy(hh, a, h + RING - REACH).wait_send()

                @pl.when(has_prev)
                def _():
                    back_copy(hh, a, h).wait_send()

        return 0

    lax.fori_loop(0, REACH, drain_halo, 0)

    for n in range(2):
        landed(k_buf, out_send.at[n])
        landed(results.at[pl.ds(2 * n, 2)], out_recv.at[n])


def write_out(landing, *refs):
    targets, sems = refs[:4], refs[4]
    copies = [
        pltpu.make_async_copy(landing.at[a], targets[a], sems.at[a]) for a in range(4)
    ]
    for copy in copies:
        copy.start()
    for copy in copies:
        copy.wait()


def solution(mesh):
    n_blk = mesh.shape["blk"]

    def on_device(queries, key_rows, value_rows, out_grad, doc_lengths):
        tok, width = queries.shape
        group_rows, keys = RING * tok, (RING + REACH) * tok
        halo, window = REACH * tok, (REACH + 1) * tok
        low, full = jnp.bfloat16, jnp.float32
        dma = pltpu.SemaphoreType.DMA
        landing = pltpu.VMEM((4, tok, width), low)
        out = jax.ShapeDtypeStruct((tok, width), low)
        any_space = pl.BlockSpec(memory_space=pl.ANY)
        flops = 6 * 2 * HEADS_EACH * RING * tok * window * HEAD_DIM
        results = pl.pallas_call(
            functools.partial(kernel, n_blk, tok),
            out_shape=landing,
            in_specs=[any_space] * 5,
            out_specs=any_space,
            scratch_shapes=[
                pltpu.VMEM((HEADS_EACH, keys, HEAD_DIM), low),
                pltpu.VMEM((HEADS_EACH, keys, HEAD_DIM), low),
                pltpu.VMEM((HEADS_EACH, group_rows, HEAD_DIM), low),
                pltpu.VMEM((HEADS_EACH, group_rows, HEAD_DIM), low),
                pltpu.VMEM((HEAD_DIM, keys), low),
                pltpu.VMEM((HEAD_DIM, keys), low),
                pltpu.VMEM((RING, tok), jnp.int32),
                pltpu.VMEM((window, tok), full),
                pltpu.VMEM((window, tok), full),
                pltpu.VMEM((window, tok), low),
                pltpu.VMEM((window, tok), low),
                pltpu.VMEM((keys, HEAD_DIM), full),
                pltpu.VMEM((keys, HEAD_DIM), full),
                pltpu.VMEM((HEADS_EACH, 4, group_rows, HEAD_DIM), low),
                pltpu.VMEM((HEADS_EACH, 2, halo, HEAD_DIM), low),
                pltpu.VMEM((HEADS_EACH, 2, halo, HEAD_DIM), low),
                dma((HEADS_EACH, 4, RING)),
                dma((HEADS_EACH, 4, RING)),
                dma((HEADS_EACH, 2, REACH)),
                dma((HEADS_EACH, 2, REACH)),
                dma((HEADS_EACH, 2, REACH)),
                dma((HEADS_EACH, 2, REACH)),
                dma((2,)),
                dma((2,)),
                pltpu.SMEM(doc_lengths.shape, jnp.int32),
                dma(()),
            ],
            compiler_params=pltpu.CompilerParams(
                collective_id=0, has_side_effects=True, vmem_limit_bytes=58 * 2**20
            ),
            cost_estimate=pl.CostEstimate(
                flops=flops, bytes_accessed=16 * tok * width, transcendentals=0
            ),
        )(doc_lengths, queries, key_rows, value_rows, out_grad)
        return pl.pallas_call(
            write_out,
            out_shape=[out] * 4,
            in_specs=[any_space],
            out_specs=[any_space] * 4,
            scratch_shapes=[dma((4,))],
            compiler_params=pltpu.CompilerParams(vmem_limit_bytes=2**20),
            cost_estimate=pl.CostEstimate(
                flops=0, bytes_accessed=16 * tok * width, transcendentals=0
            ),
        )(pltpu.with_memory_space_constraint(results, pltpu.VMEM))

    rows_spec = P(("dp", "blk"), None)
    return jax.shard_map(
        on_device,
        mesh=mesh,
        in_specs=(rows_spec,) * 4 + (P("dp"),),
        out_specs=(rows_spec,) * 4,
        check_vma=False,
    )
```

```python
import functools
import math

import jax
import jax.numpy as jnp
from jax import lax
from jax.experimental import pallas as pl
from jax.experimental.pallas import tpu as pltpu
from jax.sharding import PartitionSpec as P

HEAD_DIM = 128
REACH = 6
RING = 8
HEADS_EACH = 2
WINDOW = 12
NEG_FILL = -1e30
SCALE = 1.0 / math.sqrt(HEAD_DIM)
SCALE_LOG2 = SCALE * math.log2(math.e)
MESH = pl.DeviceIdType.MESH


def dot_nt(a, b):
    return lax.dot_general(a, b, (((1,), (1,)), ((), ())), preferred_element_type=jnp.float32)


def dot_nn(a, b):
    return jnp.dot(a, b, preferred_element_type=jnp.float32)


def kernel(
    n_blk, tok,
    doc_lengths_in, q_in, k_in, v_in, g_in,
    results,
    k_buf, v_buf, q_buf, g_buf, kt, vt, start_ref,
    s_ref, d_ref, p_ref, ds_ref, acc_k, acc_v,
    stage, halo_send, halo_recv,
    in_send, in_recv, fwd_send, fwd_recv, back_send, back_recv, out_send, out_recv,
    doc_lengths, doc_sem, met,
):
    me = lax.axis_index("blk")
    group, rank = me // RING, lax.rem(me, RING)
    n_groups = n_blk // RING
    window = (REACH + 1) * tok
    halo = REACH * tok

    def ring_device(member):
        return {"blk": group * RING + member}

    has_prev, has_next = group > 0, group < n_groups - 1
    next_device = {"blk": lax.rem(group + 1, n_groups) * RING + rank}
    prev_device = {"blk": lax.rem(group + n_groups - 1, n_groups) * RING + rank}

    def member(k):
        return lax.rem(rank + k + RING, RING)

    def head_cols(owner, hh):
        return pl.ds(pl.multiple_of((owner * HEADS_EACH + hh) * HEAD_DIM, HEAD_DIM), HEAD_DIM)

    def rows(shard):
        return pl.ds(pl.multiple_of(shard * tok, tok), tok)

    def landed(ref, sem):
        pltpu.make_async_copy(ref, ref, sem).wait()

    sources = (k_in, v_in, q_in, g_in)

    def slot(hh, a, shard):
        if a < 2:
            return (k_buf, v_buf)[a].at[hh, rows(shard + REACH), :]
        return (q_buf, g_buf)[a - 2].at[hh, rows(shard), :]

    def in_copy(hh, a, target):
        return pltpu.make_async_remote_copy(
            src_ref=sources[a].at[:, head_cols(target, hh)],
            dst_ref=slot(hh, a, rank),
            send_sem=in_send.at[hh, a, target],
            recv_sem=in_recv.at[hh, a, rank],
            device_id=ring_device(target),
            device_id_type=MESH,
        )

    def own_copy(hh, a):
        return pltpu.make_async_copy(
            sources[a].at[:, head_cols(rank, hh)], slot(hh, a, rank), in_recv.at[hh, a, rank]
        )

    def in_landed(hh, a, shard):
        landed(slot(hh, a, shard), in_recv.at[hh, a, shard])

    def fwd_copy(hh, a, shard):
        h = shard - (RING - REACH)
        return pltpu.make_async_remote_copy(
            src_ref=slot(hh, a, shard),
            dst_ref=(k_buf, v_buf)[a].at[hh, rows(h), :],
            send_sem=fwd_send.at[hh, a, h],
            recv_sem=fwd_recv.at[hh, a, h],
            device_id=next_device,
            device_id_type=MESH,
        )

    def forward(hh, shard):
        for a in range(2):
            in_landed(hh, a, shard)

        @pl.when((shard >= RING - REACH) & has_next)
        def _():
            for a in range(2):
                fwd_copy(hh, a, shard).start()

    def back_copy(hh, a, h):
        return pltpu.make_async_remote_copy(
            src_ref=halo_send.at[hh, a, rows(h), :],
            dst_ref=halo_recv.at[hh, a, rows(h), :],
            send_sem=back_send.at[hh, a, h],
            recv_sem=back_recv.at[hh, a, h],
            device_id=prev_device,
            device_id_type=MESH,
        )

    def out_pair(hh, first, target):
        pair = pl.ds(first, 2)
        return stage.at[hh, pair, rows(target), :], results.at[pair, :, head_cols(rank, hh)]

    def send_results(hh, first, target):
        source, landing = out_pair(hh, first, target)

        @pl.when(target != rank)
        def _():
            pltpu.make_async_remote_copy(
                src_ref=source,
                dst_ref=landing,
                send_sem=out_send.at[first // 2],
                recv_sem=out_recv.at[first // 2],
                device_id=ring_device(target),
                device_id_type=MESH,
            ).start()

        @pl.when(target == rank)
        def _():
            pltpu.make_async_copy(source, landing, out_recv.at[first // 2]).start()

    barrier = pltpu.get_barrier_semaphore()
    for k in range(1, RING):
        pl.semaphore_signal(barrier, inc=1, device_id=ring_device(member(k)), device_id_type=MESH)

    even = lax.rem(group, 2) == 0
    neighbours = has_next.astype(jnp.int32) + has_prev.astype(jnp.int32)

    def greet(semaphore, when):
        for present, device in ((has_next, next_device), (has_prev, prev_device)):

            @pl.when(present & when)
            def _():
                pl.semaphore_signal(semaphore, inc=1, device_id=device, device_id_type=MESH)

    greet(barrier, even)
    doc_copy = pltpu.make_async_copy(doc_lengths_in, doc_lengths, doc_sem)
    doc_copy.start()
    pl.semaphore_wait(barrier, RING - 1 + jnp.where(even, 0, neighbours))
    greet(met, jnp.logical_not(even))

    sends = [(hh, a, k) for hh in range(HEADS_EACH) for a in (0, 2) for k in range(1, RING)]
    paced = (2 * HEADS_EACH - 1) * (RING - 1)

    def start_send(n):
        hh, a, k = sends[n]
        for b in (a, a + 1):
            in_copy(hh, b, member(k)).start()

    def wait_send(n):
        hh, a, k = sends[n]
        for b in (a, a + 1):
            in_copy(hh, b, member(k)).wait_send()

    for n in range(WINDOW):
        start_send(n)
    for hh in range(HEADS_EACH):
        for a in range(4):
            own_copy(hh, a).start()

    @pl.when(jnp.logical_not(has_prev))
    def _():
        for buf in (k_buf, v_buf):
            buf[:, :halo, :] = jnp.zeros((HEADS_EACH, halo, HEAD_DIM), buf.dtype)

    @pl.when(jnp.logical_not(has_next))
    def _():
        halo_recv[...] = jnp.zeros_like(halo_recv)

    position = group * RING * tok + (
        lax.broadcasted_iota(jnp.int32, (RING, tok), 0) * tok
        + lax.broadcasted_iota(jnp.int32, (RING, tok), 1)
    )
    doc_copy.wait()
    first_key = jnp.zeros((RING, tok), jnp.int32)
    doc_end = jnp.int32(0)
    for j in range(doc_lengths.shape[0]):
        doc_end = doc_end + doc_lengths[j]
        first_key = jnp.where(position >= doc_end, doc_end, first_key)
    window_base = group * RING * tok - halo + lax.broadcasted_iota(jnp.int32, (RING, tok), 0) * tok
    start_ref[...] = first_key - window_base

    @pl.when(even)
    def _():
        pl.semaphore_wait(met, neighbours)

    forward(0, rank)

    for n in range(WINDOW, paced):
        wait_send(n - WINDOW)
        start_send(n)
        if n - WINDOW < RING - 1:
            forward(0, member(-(n - WINDOW + 1)))
    forward(1, rank)

    def transposed(hh, shard):
        kt[:, rows(shard)] = k_buf[hh, rows(shard), :].T
        vt[:, rows(shard)] = v_buf[hh, rows(shard), :].T

    key_row = lax.broadcasted_iota(jnp.int32, (tok, tok), 0)
    query_col = lax.broadcasted_iota(jnp.int32, (tok, tok), 1)

    def attend(hh, i):
        win = pl.ds(pl.multiple_of(i * tok, tok), window)
        q = q_buf[hh, rows(i), :]
        g = g_buf[hh, rows(i), :]
        start = start_ref[pl.ds(i, 1), :]
        s_ref[...] = dot_nt(k_buf[hh, win, :], q)
        top = None
        for b in range(REACH + 1):
            block = pl.ds(b * tok, tok)
            allowed = key_row >= start - b * tok
            if b == REACH:
                allowed = allowed & (key_row <= query_col)
            s = jnp.where(allowed, s_ref[block, :], NEG_FILL)
            s_ref[block, :] = s
            block_top = jnp.max(s, axis=0, keepdims=True)
            top = block_top if top is None else jnp.maximum(top, block_top)
        top = top * SCALE_LOG2
        total = None
        for b in range(REACH + 1):
            block = pl.ds(b * tok, tok)
            p = jnp.exp2(s_ref[block, :] * SCALE_LOG2 - top)
            s_ref[block, :] = p
            block_total = jnp.sum(p, axis=0, keepdims=True)
            total = block_total if total is None else total + block_total
        inverse = 1.0 / total
        for b in range(REACH + 1):
            block = pl.ds(b * tok, tok)
            p = s_ref[block, :] * inverse
            s_ref[block, :] = p
            p_ref[block, :] = p.astype(jnp.bfloat16)
        attended = dot_nn(vt[:, win], p_ref[...]).astype(jnp.bfloat16)
        stage[hh, 0, rows(i), :] = attended.T
        delta = jnp.sum(
            attended.astype(jnp.float32) * g.T.astype(jnp.float32), axis=0, keepdims=True
        )
        d_ref[...] = dot_nt(v_buf[hh, win, :], g)
        for b in range(REACH + 1):
            block = pl.ds(b * tok, tok)
            ds_ref[block, :] = (s_ref[block, :] * (d_ref[block, :] - delta)).astype(jnp.bfloat16)
        dq = dot_nn(kt[:, win], ds_ref[...]) * SCALE
        acc_k[win, :] += dot_nn(ds_ref[...], q)
        acc_v[win, :] += dot_nn(p_ref[...], g)
        stage[hh, 1, rows(i), :] = dq.astype(jnp.bfloat16).T

    def step(t, _):
        hh, i = t // RING, lax.rem(t, RING)

        @pl.when(i == 0)
        def _():
            acc_k[...] = jnp.zeros_like(acc_k)
            acc_v[...] = jnp.zeros_like(acc_v)

            def one(h, _):
                @pl.when(has_prev)
                def _():
                    landed(k_buf.at[hh, rows(h), :], fwd_recv.at[hh, 0, h])
                    landed(v_buf.at[hh, rows(h), :], fwd_recv.at[hh, 1, h])

                transposed(hh, h)
                return 0

            lax.fori_loop(0, REACH, one, 0)

        @pl.when(t * 2 < RING - 1)
        def _():
            for n in range(2):
                k = t * 2 + n + 1

                @pl.when(k < RING)
                def _():
                    for a in (2, 3):
                        in_copy(1, a, member(k)).start()

        @pl.when((t >= 1) & (t < RING))
        def _():
            forward(1, member(-t))

        for a in (2, 3):
            in_landed(hh, a, i)
        transposed(hh, i + REACH)
        attend(hh, i)
        send_results(hh, 0, i)

        @pl.when((i < REACH) & has_prev)
        def _():
            halo_send[hh, 0, rows(i), :] = (acc_k[rows(i), :] * SCALE).astype(jnp.bfloat16)
            halo_send[hh, 1, rows(i), :] = acc_v[rows(i), :].astype(jnp.bfloat16)
            for a in range(2):
                back_copy(hh, a, i).start()

        @pl.when(i == RING - 1)
        def _():
            def finish(k, _):
                shard = k

                def put(dk, dv):
                    stage[hh, 2, rows(shard), :] = dk.astype(jnp.bfloat16)
                    stage[hh, 3, rows(shard), :] = dv.astype(jnp.bfloat16)

                own = rows(shard + REACH)

                @pl.when(shard < RING - REACH)
                def _():
                    put(acc_k[own, :] * SCALE, acc_v[own, :])

                @pl.when(shard >= RING - REACH)
                def _():
                    h = shard - (RING - REACH)

                    @pl.when(has_next)
                    def _():
                        for a in range(2):
                            landed(halo_recv.at[hh, a, rows(h), :], back_recv.at[hh, a, h])

                    put(
                        acc_k[own, :] * SCALE + halo_recv[hh, 0, rows(h), :].astype(jnp.float32),
                        acc_v[own, :] + halo_recv[hh, 1, rows(h), :].astype(jnp.float32),
                    )

                send_results(hh, 2, shard)
                return 0

            lax.fori_loop(0, RING, finish, 0)

        return 0

    lax.fori_loop(0, HEADS_EACH * RING, step, 0)

    for n in range(paced - WINDOW, len(sends)):
        wait_send(n)
    def drain_halo(h, _):
        for hh in range(HEADS_EACH):
            for a in range(2):
                @pl.when(has_next)
                def _():
                    fwd_copy(hh, a, h + RING - REACH).wait_send()

                @pl.when(has_prev)
                def _():
                    back_copy(hh, a, h).wait_send()

        return 0

    lax.fori_loop(0, REACH, drain_halo, 0)

    for n in range(2):
        landed(k_buf, out_send.at[n])
        landed(results.at[pl.ds(2 * n, 2)], out_recv.at[n])


def write_out(landing, *refs):
    targets, sems = refs[:4], refs[4]
    copies = [
        pltpu.make_async_copy(landing.at[a], targets[a], sems.at[a]) for a in range(4)
    ]
    for copy in copies:
        copy.start()
    for copy in copies:
        copy.wait()


def solution(mesh):
    n_blk = mesh.shape["blk"]

    def on_device(queries, key_rows, value_rows, out_grad, doc_lengths):
        tok, width = queries.shape
        group_rows, keys = RING * tok, (RING + REACH) * tok
        halo, window = REACH * tok, (REACH + 1) * tok
        low, full = jnp.bfloat16, jnp.float32
        dma = pltpu.SemaphoreType.DMA
        landing = pltpu.VMEM((4, tok, width), low)
        out = jax.ShapeDtypeStruct((tok, width), low)
        any_space = pl.BlockSpec(memory_space=pl.ANY)
        flops = 6 * 2 * HEADS_EACH * RING * tok * window * HEAD_DIM
        results = pl.pallas_call(
            functools.partial(kernel, n_blk, tok),
            out_shape=landing,
            in_specs=[any_space] * 5,
            out_specs=any_space,
            scratch_shapes=[
                pltpu.VMEM((HEADS_EACH, keys, HEAD_DIM), low),
                pltpu.VMEM((HEADS_EACH, keys, HEAD_DIM), low),
                pltpu.VMEM((HEADS_EACH, group_rows, HEAD_DIM), low),
                pltpu.VMEM((HEADS_EACH, group_rows, HEAD_DIM), low),
                pltpu.VMEM((HEAD_DIM, keys), low),
                pltpu.VMEM((HEAD_DIM, keys), low),
                pltpu.VMEM((RING, tok), jnp.int32),
                pltpu.VMEM((window, tok), full),
                pltpu.VMEM((window, tok), full),
                pltpu.VMEM((window, tok), low),
                pltpu.VMEM((window, tok), low),
                pltpu.VMEM((keys, HEAD_DIM), full),
                pltpu.VMEM((keys, HEAD_DIM), full),
                pltpu.VMEM((HEADS_EACH, 4, group_rows, HEAD_DIM), low),
                pltpu.VMEM((HEADS_EACH, 2, halo, HEAD_DIM), low),
                pltpu.VMEM((HEADS_EACH, 2, halo, HEAD_DIM), low),
                dma((HEADS_EACH, 4, RING)),
                dma((HEADS_EACH, 4, RING)),
                dma((HEADS_EACH, 2, REACH)),
                dma((HEADS_EACH, 2, REACH)),
                dma((HEADS_EACH, 2, REACH)),
                dma((HEADS_EACH, 2, REACH)),
                dma((2,)),
                dma((2,)),
                pltpu.SMEM(doc_lengths.shape, jnp.int32),
                dma(()),
                pltpu.SemaphoreType.REGULAR,
            ],
            compiler_params=pltpu.CompilerParams(
                collective_id=0, has_side_effects=True, vmem_limit_bytes=58 * 2**20
            ),
            cost_estimate=pl.CostEstimate(
                flops=flops, bytes_accessed=16 * tok * width, transcendentals=0
            ),
        )(doc_lengths, queries, key_rows, value_rows, out_grad)
        return pl.pallas_call(
            write_out,
            out_shape=[out] * 4,
            in_specs=[any_space],
            out_specs=[any_space] * 4,
            scratch_shapes=[dma((4,))],
            compiler_params=pltpu.CompilerParams(vmem_limit_bytes=2**20),
            cost_estimate=pl.CostEstimate(
                flops=0, bytes_accessed=16 * tok * width, transcendentals=0
            ),
        )(pltpu.with_memory_space_constraint(results, pltpu.VMEM))

    rows_spec = P(("dp", "blk"), None)
    return jax.shard_map(
        on_device,
        mesh=mesh,
        in_specs=(rows_spec,) * 4 + (P("dp"),),
        out_specs=(rows_spec,) * 4,
        check_vma=False,
    )
```

```python
import functools
import math

import jax
import jax.numpy as jnp
from jax import lax
from jax.experimental import pallas as pl
from jax.experimental.pallas import tpu as pltpu
from jax.sharding import PartitionSpec as P

HEAD_DIM = 128
REACH = 6
RING = 8
HEADS_EACH = 2
WINDOW = 12
NEG_FILL = -1e30
SCALE = 1.0 / math.sqrt(HEAD_DIM)
SCALE_LOG2 = SCALE * math.log2(math.e)
MESH = pl.DeviceIdType.MESH


def dot_nt(a, b):
    return lax.dot_general(a, b, (((1,), (1,)), ((), ())), preferred_element_type=jnp.float32)


def dot_nn(a, b):
    return jnp.dot(a, b, preferred_element_type=jnp.float32)


def kernel(
    n_blk, tok,
    doc_lengths_in, q_in, k_in, v_in, g_in,
    results,
    k_buf, v_buf, q_buf, g_buf, kt, vt, start_ref,
    s_ref, d_ref, p_ref, ds_ref, acc_k, acc_v,
    stage, halo_send, halo_recv,
    in_send, in_recv, fwd_send, fwd_recv, back_send, back_recv, out_send, out_recv,
    doc_lengths, doc_sem, met,
):
    me = lax.axis_index("blk")
    group, rank = me // RING, lax.rem(me, RING)
    n_groups = n_blk // RING
    window = (REACH + 1) * tok
    halo = REACH * tok

    def ring_device(member):
        return {"blk": group * RING + member}

    has_prev, has_next = group > 0, group < n_groups - 1
    next_device = {"blk": lax.rem(group + 1, n_groups) * RING + rank}
    prev_device = {"blk": lax.rem(group + n_groups - 1, n_groups) * RING + rank}

    def member(k):
        return lax.rem(rank + k + RING, RING)

    def head_cols(owner, hh):
        return pl.ds(pl.multiple_of((owner * HEADS_EACH + hh) * HEAD_DIM, HEAD_DIM), HEAD_DIM)

    def rows(shard):
        return pl.ds(pl.multiple_of(shard * tok, tok), tok)

    def landed(ref, sem):
        pltpu.make_async_copy(ref, ref, sem).wait()

    sources = (k_in, v_in, q_in, g_in)

    def slot(hh, a, shard):
        if a < 2:
            return (k_buf, v_buf)[a].at[hh, rows(shard + REACH), :]
        return (q_buf, g_buf)[a - 2].at[hh, rows(shard), :]

    def in_copy(hh, a, target):
        return pltpu.make_async_remote_copy(
            src_ref=sources[a].at[:, head_cols(target, hh)],
            dst_ref=slot(hh, a, rank),
            send_sem=in_send.at[hh, a, target],
            recv_sem=in_recv.at[hh, a, rank],
            device_id=ring_device(target),
            device_id_type=MESH,
        )

    def own_copy(hh, a):
        return pltpu.make_async_copy(
            sources[a].at[:, head_cols(rank, hh)], slot(hh, a, rank), in_recv.at[hh, a, rank]
        )

    def in_landed(hh, a, shard):
        landed(slot(hh, a, shard), in_recv.at[hh, a, shard])

    def fwd_copy(hh, a, shard):
        h = shard - (RING - REACH)
        return pltpu.make_async_remote_copy(
            src_ref=slot(hh, a, shard),
            dst_ref=(k_buf, v_buf)[a].at[hh, rows(h), :],
            send_sem=fwd_send.at[hh, a, h],
            recv_sem=fwd_recv.at[hh, a, h],
            device_id=next_device,
            device_id_type=MESH,
        )

    def forward(hh, shard):
        for a in range(2):
            in_landed(hh, a, shard)

        @pl.when((shard >= RING - REACH) & has_next)
        def _():
            for a in range(2):
                fwd_copy(hh, a, shard).start()

    def back_copy(hh, a, h):
        return pltpu.make_async_remote_copy(
            src_ref=halo_send.at[hh, a, rows(h), :],
            dst_ref=halo_recv.at[hh, a, rows(h), :],
            send_sem=back_send.at[hh, a, h],
            recv_sem=back_recv.at[hh, a, h],
            device_id=prev_device,
            device_id_type=MESH,
        )

    def out_pair(hh, first, target):
        pair = pl.ds(first, 2)
        return stage.at[hh, pair, rows(target), :], results.at[pair, :, head_cols(rank, hh)]

    def send_results(hh, first, target):
        source, landing = out_pair(hh, first, target)

        @pl.when(target != rank)
        def _():
            pltpu.make_async_remote_copy(
                src_ref=source,
                dst_ref=landing,
                send_sem=out_send.at[first // 2],
                recv_sem=out_recv.at[first // 2],
                device_id=ring_device(target),
                device_id_type=MESH,
            ).start()

        @pl.when(target == rank)
        def _():
            pltpu.make_async_copy(source, landing, out_recv.at[first // 2]).start()

    barrier = pltpu.get_barrier_semaphore()
    for k in range(1, RING):
        pl.semaphore_signal(barrier, inc=1, device_id=ring_device(member(k)), device_id_type=MESH)

    even = lax.rem(group, 2) == 0
    neighbours = has_next.astype(jnp.int32) + has_prev.astype(jnp.int32)

    def greet(semaphore, when):
        for present, device in ((has_next, next_device), (has_prev, prev_device)):

            @pl.when(present & when)
            def _():
                pl.semaphore_signal(semaphore, inc=1, device_id=device, device_id_type=MESH)

    greet(barrier, even)
    doc_copy = pltpu.make_async_copy(doc_lengths_in, doc_lengths, doc_sem)
    doc_copy.start()
    pl.semaphore_wait(barrier, RING - 1 + jnp.where(even, 0, neighbours))
    greet(met, jnp.logical_not(even))

    sends = [(hh, a, k) for hh in range(HEADS_EACH) for a in (0, 2) for k in range(1, RING)]
    paced = (2 * HEADS_EACH - 1) * (RING - 1)

    def start_send(n):
        hh, a, k = sends[n]
        for b in (a, a + 1):
            in_copy(hh, b, member(k)).start()

    def wait_send(n):
        hh, a, k = sends[n]
        for b in (a, a + 1):
            in_copy(hh, b, member(k)).wait_send()

    for n in range(WINDOW):
        start_send(n)
    for hh in range(HEADS_EACH):
        for a in range(4):
            own_copy(hh, a).start()

    @pl.when(jnp.logical_not(has_prev))
    def _():
        for buf in (k_buf, v_buf):
            buf[:, :halo, :] = jnp.zeros((HEADS_EACH, halo, HEAD_DIM), buf.dtype)

    @pl.when(jnp.logical_not(has_next))
    def _():
        halo_recv[...] = jnp.zeros_like(halo_recv)

    position = group * RING * tok + (
        lax.broadcasted_iota(jnp.int32, (RING, tok), 0) * tok
        + lax.broadcasted_iota(jnp.int32, (RING, tok), 1)
    )
    doc_copy.wait()
    first_key = jnp.zeros((RING, tok), jnp.int32)
    doc_end = jnp.int32(0)
    for j in range(doc_lengths.shape[0]):
        doc_end = doc_end + doc_lengths[j]
        first_key = jnp.where(position >= doc_end, doc_end, first_key)
    window_base = group * RING * tok - halo + lax.broadcasted_iota(jnp.int32, (RING, tok), 0) * tok
    start_ref[...] = first_key - window_base

    @pl.when(even)
    def _():
        pl.semaphore_wait(met, neighbours)

    forward(0, rank)

    for n in range(WINDOW, paced):
        wait_send(n - WINDOW)
        start_send(n)
        if n - WINDOW < RING - 1:
            forward(0, member(-(n - WINDOW + 1)))
    forward(1, rank)

    def transposed(hh, shard):
        kt[:, rows(shard)] = k_buf[hh, rows(shard), :].T
        vt[:, rows(shard)] = v_buf[hh, rows(shard), :].T

    key_row = lax.broadcasted_iota(jnp.int32, (tok, tok), 0)
    query_col = lax.broadcasted_iota(jnp.int32, (tok, tok), 1)

    def attend(hh, i):
        win = pl.ds(pl.multiple_of(i * tok, tok), window)
        q = q_buf[hh, rows(i), :]
        g = g_buf[hh, rows(i), :]
        start = start_ref[pl.ds(i, 1), :]
        s_ref[...] = dot_nt(k_buf[hh, win, :], q)
        top = None
        for b in range(REACH + 1):
            block = pl.ds(b * tok, tok)
            allowed = key_row >= start - b * tok
            if b == REACH:
                allowed = allowed & (key_row <= query_col)
            s = jnp.where(allowed, s_ref[block, :], NEG_FILL)
            s_ref[block, :] = s
            block_top = jnp.max(s, axis=0, keepdims=True)
            top = block_top if top is None else jnp.maximum(top, block_top)
        top = top * SCALE_LOG2
        total = None
        for b in range(REACH + 1):
            block = pl.ds(b * tok, tok)
            p = jnp.exp2(s_ref[block, :] * SCALE_LOG2 - top)
            s_ref[block, :] = p
            block_total = jnp.sum(p, axis=0, keepdims=True)
            total = block_total if total is None else total + block_total
        inverse = 1.0 / total
        for b in range(REACH + 1):
            block = pl.ds(b * tok, tok)
            p = s_ref[block, :] * inverse
            s_ref[block, :] = p
            p_ref[block, :] = p.astype(jnp.bfloat16)
        attended = dot_nn(vt[:, win], p_ref[...]).astype(jnp.bfloat16)
        stage[hh, 0, rows(i), :] = attended.T
        delta = jnp.sum(
            attended.astype(jnp.float32) * g.T.astype(jnp.float32), axis=0, keepdims=True
        )
        d_ref[...] = dot_nt(v_buf[hh, win, :], g)
        for b in range(REACH + 1):
            block = pl.ds(b * tok, tok)
            ds_ref[block, :] = (s_ref[block, :] * (d_ref[block, :] - delta)).astype(jnp.bfloat16)
        dq = dot_nn(kt[:, win], ds_ref[...]) * SCALE
        acc_k[win, :] += dot_nn(ds_ref[...], q)
        acc_v[win, :] += dot_nn(p_ref[...], g)
        stage[hh, 1, rows(i), :] = dq.astype(jnp.bfloat16).T

    def step(t, _):
        hh, i = t // RING, lax.rem(t, RING)

        @pl.when(i == 0)
        def _():
            acc_k[...] = jnp.zeros_like(acc_k)
            acc_v[...] = jnp.zeros_like(acc_v)

            def one(h, _):
                @pl.when(has_prev)
                def _():
                    landed(k_buf.at[hh, rows(h), :], fwd_recv.at[hh, 0, h])
                    landed(v_buf.at[hh, rows(h), :], fwd_recv.at[hh, 1, h])

                transposed(hh, h)
                return 0

            lax.fori_loop(0, REACH, one, 0)

        @pl.when(t * 2 < RING - 1)
        def _():
            for n in range(2):
                k = t * 2 + n + 1

                @pl.when(k < RING)
                def _():
                    for a in (2, 3):
                        in_copy(1, a, member(k)).start()

        @pl.when((t >= 1) & (t < RING))
        def _():
            forward(1, member(-t))

        for a in (2, 3):
            in_landed(hh, a, i)
        transposed(hh, i + REACH)
        attend(hh, i)
        send_results(hh, 0, i)

        @pl.when((i < REACH) & has_prev)
        def _():
            halo_send[hh, 0, rows(i), :] = (acc_k[rows(i), :] * SCALE).astype(jnp.bfloat16)
            halo_send[hh, 1, rows(i), :] = acc_v[rows(i), :].astype(jnp.bfloat16)
            for a in range(2):
                back_copy(hh, a, i).start()

        def finish(shard, _):

            def put(dk, dv):
                stage[hh, 2, rows(shard), :] = dk.astype(jnp.bfloat16)
                stage[hh, 3, rows(shard), :] = dv.astype(jnp.bfloat16)

            own = rows(shard + REACH)

            @pl.when(shard < RING - REACH)
            def _():
                put(acc_k[own, :] * SCALE, acc_v[own, :])

            @pl.when(shard >= RING - REACH)
            def _():
                h = shard - (RING - REACH)

                @pl.when(has_next)
                def _():
                    for a in range(2):
                        landed(halo_recv.at[hh, a, rows(h), :], back_recv.at[hh, a, h])

                put(
                    acc_k[own, :] * SCALE + halo_recv[hh, 0, rows(h), :].astype(jnp.float32),
                    acc_v[own, :] + halo_recv[hh, 1, rows(h), :].astype(jnp.float32),
                )

            send_results(hh, 2, shard)
            return 0

        @pl.when(i == RING - 2)
        def _():
            finish(jnp.int32(0), 0)

        @pl.when(i == RING - 1)
        def _():
            lax.fori_loop(1, RING, finish, 0)

        return 0

    lax.fori_loop(0, HEADS_EACH * RING, step, 0)

    for n in range(paced - WINDOW, len(sends)):
        wait_send(n)
    def drain_halo(h, _):
        for hh in range(HEADS_EACH):
            for a in range(2):
                @pl.when(has_next)
                def _():
                    fwd_copy(hh, a, h + RING - REACH).wait_send()

                @pl.when(has_prev)
                def _():
                    back_copy(hh, a, h).wait_send()

        return 0

    lax.fori_loop(0, REACH, drain_halo, 0)

    for n in range(2):
        landed(k_buf, out_send.at[n])
        landed(results.at[pl.ds(2 * n, 2)], out_recv.at[n])


def write_out(landing, *refs):
    targets, sems = refs[:4], refs[4]
    copies = [
        pltpu.make_async_copy(landing.at[a], targets[a], sems.at[a]) for a in range(4)
    ]
    for copy in copies:
        copy.start()
    for copy in copies:
        copy.wait()


def solution(mesh):
    n_blk = mesh.shape["blk"]

    def on_device(queries, key_rows, value_rows, out_grad, doc_lengths):
        tok, width = queries.shape
        group_rows, keys = RING * tok, (RING + REACH) * tok
        halo, window = REACH * tok, (REACH + 1) * tok
        low, full = jnp.bfloat16, jnp.float32
        dma = pltpu.SemaphoreType.DMA
        landing = pltpu.VMEM((4, tok, width), low)
        out = jax.ShapeDtypeStruct((tok, width), low)
        any_space = pl.BlockSpec(memory_space=pl.ANY)
        flops = 6 * 2 * HEADS_EACH * RING * tok * window * HEAD_DIM
        results = pl.pallas_call(
            functools.partial(kernel, n_blk, tok),
            out_shape=landing,
            in_specs=[any_space] * 5,
            out_specs=any_space,
            scratch_shapes=[
                pltpu.VMEM((HEADS_EACH, keys, HEAD_DIM), low),
                pltpu.VMEM((HEADS_EACH, keys, HEAD_DIM), low),
                pltpu.VMEM((HEADS_EACH, group_rows, HEAD_DIM), low),
                pltpu.VMEM((HEADS_EACH, group_rows, HEAD_DIM), low),
                pltpu.VMEM((HEAD_DIM, keys), low),
                pltpu.VMEM((HEAD_DIM, keys), low),
                pltpu.VMEM((RING, tok), jnp.int32),
                pltpu.VMEM((window, tok), full),
                pltpu.VMEM((window, tok), full),
                pltpu.VMEM((window, tok), low),
                pltpu.VMEM((window, tok), low),
                pltpu.VMEM((keys, HEAD_DIM), full),
                pltpu.VMEM((keys, HEAD_DIM), full),
                pltpu.VMEM((HEADS_EACH, 4, group_rows, HEAD_DIM), low),
                pltpu.VMEM((HEADS_EACH, 2, halo, HEAD_DIM), low),
                pltpu.VMEM((HEADS_EACH, 2, halo, HEAD_DIM), low),
                dma((HEADS_EACH, 4, RING)),
                dma((HEADS_EACH, 4, RING)),
                dma((HEADS_EACH, 2, REACH)),
                dma((HEADS_EACH, 2, REACH)),
                dma((HEADS_EACH, 2, REACH)),
                dma((HEADS_EACH, 2, REACH)),
                dma((2,)),
                dma((2,)),
                pltpu.SMEM(doc_lengths.shape, jnp.int32),
                dma(()),
                pltpu.SemaphoreType.REGULAR,
            ],
            compiler_params=pltpu.CompilerParams(
                collective_id=0, has_side_effects=True, vmem_limit_bytes=58 * 2**20
            ),
            cost_estimate=pl.CostEstimate(
                flops=flops, bytes_accessed=16 * tok * width, transcendentals=0
            ),
        )(doc_lengths, queries, key_rows, value_rows, out_grad)
        return pl.pallas_call(
            write_out,
            out_shape=[out] * 4,
            in_specs=[any_space],
            out_specs=[any_space] * 4,
            scratch_shapes=[dma((4,))],
            compiler_params=pltpu.CompilerParams(vmem_limit_bytes=2**20),
            cost_estimate=pl.CostEstimate(
                flops=0, bytes_accessed=16 * tok * width, transcendentals=0
            ),
        )(pltpu.with_memory_space_constraint(results, pltpu.VMEM))

    rows_spec = P(("dp", "blk"), None)
    return jax.shard_map(
        on_device,
        mesh=mesh,
        in_specs=(rows_spec,) * 4 + (P("dp"),),
        out_specs=(rows_spec,) * 4,
        check_vma=False,
    )
```

```python
import functools
import math

import jax
import jax.numpy as jnp
from jax import lax
from jax.experimental import pallas as pl
from jax.experimental.pallas import tpu as pltpu
from jax.sharding import PartitionSpec as P

HEAD_DIM = 128
REACH = 6
RING = 8
HEADS_EACH = 2
WINDOW = 12
DISTANCES = (2, 6, 1, 3, 7, 5, 4)
NEG_FILL = -1e30
SCALE = 1.0 / math.sqrt(HEAD_DIM)
SCALE_LOG2 = SCALE * math.log2(math.e)
MESH = pl.DeviceIdType.MESH


def dot_nt(a, b):
    return lax.dot_general(a, b, (((1,), (1,)), ((), ())), preferred_element_type=jnp.float32)


def dot_nn(a, b):
    return jnp.dot(a, b, preferred_element_type=jnp.float32)


def kernel(
    n_blk, tok,
    doc_lengths_in, q_in, k_in, v_in, g_in,
    results,
    k_buf, v_buf, q_buf, g_buf, kt, vt, start_ref,
    s_ref, d_ref, p_ref, ds_ref, acc_k, acc_v,
    stage, halo_send, halo_recv,
    in_send, in_recv, fwd_send, fwd_recv, back_send, back_recv, out_send, out_recv,
    doc_lengths, doc_sem, met,
):
    me = lax.axis_index("blk")
    group, rank = me // RING, lax.rem(me, RING)
    n_groups = n_blk // RING
    window = (REACH + 1) * tok
    halo = REACH * tok

    def ring_device(member):
        return {"blk": group * RING + member}

    has_prev, has_next = group > 0, group < n_groups - 1
    next_device = {"blk": lax.rem(group + 1, n_groups) * RING + rank}
    prev_device = {"blk": lax.rem(group + n_groups - 1, n_groups) * RING + rank}

    def member(k):
        return lax.rem(rank + k + RING, RING)

    def head_cols(owner, hh):
        return pl.ds(pl.multiple_of((owner * HEADS_EACH + hh) * HEAD_DIM, HEAD_DIM), HEAD_DIM)

    def rows(shard):
        return pl.ds(pl.multiple_of(shard * tok, tok), tok)

    def landed(ref, sem):
        pltpu.make_async_copy(ref, ref, sem).wait()

    sources = (k_in, v_in, q_in, g_in)

    def slot(hh, a, shard):
        if a < 2:
            return (k_buf, v_buf)[a].at[hh, rows(shard + REACH), :]
        return (q_buf, g_buf)[a - 2].at[hh, rows(shard), :]

    def in_copy(hh, a, target):
        return pltpu.make_async_remote_copy(
            src_ref=sources[a].at[:, head_cols(target, hh)],
            dst_ref=slot(hh, a, rank),
            send_sem=in_send.at[hh, a, target],
            recv_sem=in_recv.at[hh, a, rank],
            device_id=ring_device(target),
            device_id_type=MESH,
        )

    def own_copy(hh, a):
        return pltpu.make_async_copy(
            sources[a].at[:, head_cols(rank, hh)], slot(hh, a, rank), in_recv.at[hh, a, rank]
        )

    def in_landed(hh, a, shard):
        landed(slot(hh, a, shard), in_recv.at[hh, a, shard])

    def fwd_copy(hh, a, shard):
        h = shard - (RING - REACH)
        return pltpu.make_async_remote_copy(
            src_ref=slot(hh, a, shard),
            dst_ref=(k_buf, v_buf)[a].at[hh, rows(h), :],
            send_sem=fwd_send.at[hh, a, h],
            recv_sem=fwd_recv.at[hh, a, h],
            device_id=next_device,
            device_id_type=MESH,
        )

    def forward(hh, shard):
        for a in range(2):
            in_landed(hh, a, shard)

        @pl.when((shard >= RING - REACH) & has_next)
        def _():
            for a in range(2):
                fwd_copy(hh, a, shard).start()

    def back_copy(hh, a, h):
        return pltpu.make_async_remote_copy(
            src_ref=halo_send.at[hh, a, rows(h), :],
            dst_ref=halo_recv.at[hh, a, rows(h), :],
            send_sem=back_send.at[hh, a, h],
            recv_sem=back_recv.at[hh, a, h],
            device_id=prev_device,
            device_id_type=MESH,
        )

    def out_pair(hh, first, target):
        pair = pl.ds(first, 2)
        return stage.at[hh, pair, rows(target), :], results.at[pair, :, head_cols(rank, hh)]

    def send_results(hh, first, target):
        source, landing = out_pair(hh, first, target)

        @pl.when(target != rank)
        def _():
            pltpu.make_async_remote_copy(
                src_ref=source,
                dst_ref=landing,
                send_sem=out_send.at[first // 2],
                recv_sem=out_recv.at[first // 2],
                device_id=ring_device(target),
                device_id_type=MESH,
            ).start()

        @pl.when(target == rank)
        def _():
            pltpu.make_async_copy(source, landing, out_recv.at[first // 2]).start()

    barrier = pltpu.get_barrier_semaphore()
    for k in range(1, RING):
        pl.semaphore_signal(barrier, inc=1, device_id=ring_device(member(k)), device_id_type=MESH)

    even = lax.rem(group, 2) == 0
    neighbours = has_next.astype(jnp.int32) + has_prev.astype(jnp.int32)

    def greet(semaphore, when):
        for present, device in ((has_next, next_device), (has_prev, prev_device)):

            @pl.when(present & when)
            def _():
                pl.semaphore_signal(semaphore, inc=1, device_id=device, device_id_type=MESH)

    greet(barrier, even)
    doc_copy = pltpu.make_async_copy(doc_lengths_in, doc_lengths, doc_sem)
    doc_copy.start()
    pl.semaphore_wait(barrier, RING - 1 + jnp.where(even, 0, neighbours))
    greet(met, jnp.logical_not(even))

    sends = [(hh, a, k) for hh in range(HEADS_EACH) for a in (0, 2) for k in DISTANCES]
    paced = (2 * HEADS_EACH - 1) * (RING - 1)

    def start_send(n):
        hh, a, k = sends[n]
        for b in (a, a + 1):
            in_copy(hh, b, member(k)).start()

    def wait_send(n):
        hh, a, k = sends[n]
        for b in (a, a + 1):
            in_copy(hh, b, member(k)).wait_send()

    for n in range(WINDOW):
        start_send(n)
    for hh in range(HEADS_EACH):
        for a in range(4):
            own_copy(hh, a).start()

    @pl.when(jnp.logical_not(has_prev))
    def _():
        for buf in (k_buf, v_buf):
            buf[:, :halo, :] = jnp.zeros((HEADS_EACH, halo, HEAD_DIM), buf.dtype)

    @pl.when(jnp.logical_not(has_next))
    def _():
        halo_recv[...] = jnp.zeros_like(halo_recv)

    position = group * RING * tok + (
        lax.broadcasted_iota(jnp.int32, (RING, tok), 0) * tok
        + lax.broadcasted_iota(jnp.int32, (RING, tok), 1)
    )
    doc_copy.wait()
    first_key = jnp.zeros((RING, tok), jnp.int32)
    doc_end = jnp.int32(0)
    for j in range(doc_lengths.shape[0]):
        doc_end = doc_end + doc_lengths[j]
        first_key = jnp.where(position >= doc_end, doc_end, first_key)
    window_base = group * RING * tok - halo + lax.broadcasted_iota(jnp.int32, (RING, tok), 0) * tok
    start_ref[...] = first_key - window_base

    @pl.when(even)
    def _():
        pl.semaphore_wait(met, neighbours)

    forward(0, rank)

    for n in range(WINDOW, paced):
        wait_send(n - WINDOW)
        start_send(n)
        if n - WINDOW < RING - 1:
            forward(0, member(-sends[n - WINDOW][2]))
    forward(1, rank)

    def transposed(hh, shard):
        kt[:, rows(shard)] = k_buf[hh, rows(shard), :].T
        vt[:, rows(shard)] = v_buf[hh, rows(shard), :].T

    key_row = lax.broadcasted_iota(jnp.int32, (tok, tok), 0)
    query_col = lax.broadcasted_iota(jnp.int32, (tok, tok), 1)

    def attend(hh, i):
        win = pl.ds(pl.multiple_of(i * tok, tok), window)
        q = q_buf[hh, rows(i), :]
        g = g_buf[hh, rows(i), :]
        start = start_ref[pl.ds(i, 1), :]
        s_ref[...] = dot_nt(k_buf[hh, win, :], q)
        top = None
        for b in range(REACH + 1):
            block = pl.ds(b * tok, tok)
            allowed = key_row >= start - b * tok
            if b == REACH:
                allowed = allowed & (key_row <= query_col)
            s = jnp.where(allowed, s_ref[block, :], NEG_FILL)
            s_ref[block, :] = s
            block_top = jnp.max(s, axis=0, keepdims=True)
            top = block_top if top is None else jnp.maximum(top, block_top)
        top = top * SCALE_LOG2
        total = None
        for b in range(REACH + 1):
            block = pl.ds(b * tok, tok)
            p = jnp.exp2(s_ref[block, :] * SCALE_LOG2 - top)
            s_ref[block, :] = p
            block_total = jnp.sum(p, axis=0, keepdims=True)
            total = block_total if total is None else total + block_total
        inverse = 1.0 / total
        for b in range(REACH + 1):
            block = pl.ds(b * tok, tok)
            p = s_ref[block, :] * inverse
            s_ref[block, :] = p
            p_ref[block, :] = p.astype(jnp.bfloat16)
        attended = dot_nn(vt[:, win], p_ref[...]).astype(jnp.bfloat16)
        stage[hh, 0, rows(i), :] = attended.T
        delta = jnp.sum(
            attended.astype(jnp.float32) * g.T.astype(jnp.float32), axis=0, keepdims=True
        )
        d_ref[...] = dot_nt(v_buf[hh, win, :], g)
        for b in range(REACH + 1):
            block = pl.ds(b * tok, tok)
            ds_ref[block, :] = (s_ref[block, :] * (d_ref[block, :] - delta)).astype(jnp.bfloat16)
        dq = dot_nn(kt[:, win], ds_ref[...]) * SCALE
        acc_k[win, :] += dot_nn(ds_ref[...], q)
        acc_v[win, :] += dot_nn(p_ref[...], g)
        stage[hh, 1, rows(i), :] = dq.astype(jnp.bfloat16).T

    def step(t, _):
        hh, i = t // RING, lax.rem(t, RING)

        @pl.when(i == 0)
        def _():
            acc_k[...] = jnp.zeros_like(acc_k)
            acc_v[...] = jnp.zeros_like(acc_v)

            def one(h, _):
                @pl.when(has_prev)
                def _():
                    landed(k_buf.at[hh, rows(h), :], fwd_recv.at[hh, 0, h])
                    landed(v_buf.at[hh, rows(h), :], fwd_recv.at[hh, 1, h])

                transposed(hh, h)
                return 0

            lax.fori_loop(0, REACH, one, 0)

        @pl.when(t * 2 < RING - 1)
        def _():
            for n in range(2):
                k = t * 2 + n + 1

                @pl.when(k < RING)
                def _():
                    for a in (2, 3):
                        in_copy(1, a, member(k)).start()

        @pl.when((t >= 1) & (t < RING))
        def _():
            forward(1, member(-t))

        for a in (2, 3):
            in_landed(hh, a, i)
        transposed(hh, i + REACH)
        attend(hh, i)
        send_results(hh, 0, i)

        @pl.when((i < REACH) & has_prev)
        def _():
            halo_send[hh, 0, rows(i), :] = (acc_k[rows(i), :] * SCALE).astype(jnp.bfloat16)
            halo_send[hh, 1, rows(i), :] = acc_v[rows(i), :].astype(jnp.bfloat16)
            for a in range(2):
                back_copy(hh, a, i).start()

        @pl.when(i == RING - 1)
        def _():
            def finish(k, _):
                shard = k

                def put(dk, dv):
                    stage[hh, 2, rows(shard), :] = dk.astype(jnp.bfloat16)
                    stage[hh, 3, rows(shard), :] = dv.astype(jnp.bfloat16)

                own = rows(shard + REACH)

                @pl.when(shard < RING - REACH)
                def _():
                    put(acc_k[own, :] * SCALE, acc_v[own, :])

                @pl.when(shard >= RING - REACH)
                def _():
                    h = shard - (RING - REACH)

                    @pl.when(has_next)
                    def _():
                        for a in range(2):
                            landed(halo_recv.at[hh, a, rows(h), :], back_recv.at[hh, a, h])

                    put(
                        acc_k[own, :] * SCALE + halo_recv[hh, 0, rows(h), :].astype(jnp.float32),
                        acc_v[own, :] + halo_recv[hh, 1, rows(h), :].astype(jnp.float32),
                    )

                send_results(hh, 2, shard)
                return 0

            lax.fori_loop(0, RING, finish, 0)

        return 0

    lax.fori_loop(0, HEADS_EACH * RING, step, 0)

    for n in range(paced - WINDOW, len(sends)):
        wait_send(n)
    def drain_halo(h, _):
        for hh in range(HEADS_EACH):
            for a in range(2):
                @pl.when(has_next)
                def _():
                    fwd_copy(hh, a, h + RING - REACH).wait_send()

                @pl.when(has_prev)
                def _():
                    back_copy(hh, a, h).wait_send()

        return 0

    lax.fori_loop(0, REACH, drain_halo, 0)

    for n in range(2):
        landed(k_buf, out_send.at[n])
        landed(results.at[pl.ds(2 * n, 2)], out_recv.at[n])


def write_out(landing, *refs):
    targets, sems = refs[:4], refs[4]
    copies = [
        pltpu.make_async_copy(landing.at[a], targets[a], sems.at[a]) for a in range(4)
    ]
    for copy in copies:
        copy.start()
    for copy in copies:
        copy.wait()


def solution(mesh):
    n_blk = mesh.shape["blk"]

    def on_device(queries, key_rows, value_rows, out_grad, doc_lengths):
        tok, width = queries.shape
        group_rows, keys = RING * tok, (RING + REACH) * tok
        halo, window = REACH * tok, (REACH + 1) * tok
        low, full = jnp.bfloat16, jnp.float32
        dma = pltpu.SemaphoreType.DMA
        landing = pltpu.VMEM((4, tok, width), low)
        out = jax.ShapeDtypeStruct((tok, width), low)
        any_space = pl.BlockSpec(memory_space=pl.ANY)
        flops = 6 * 2 * HEADS_EACH * RING * tok * window * HEAD_DIM
        results = pl.pallas_call(
            functools.partial(kernel, n_blk, tok),
            out_shape=landing,
            in_specs=[any_space] * 5,
            out_specs=any_space,
            scratch_shapes=[
                pltpu.VMEM((HEADS_EACH, keys, HEAD_DIM), low),
                pltpu.VMEM((HEADS_EACH, keys, HEAD_DIM), low),
                pltpu.VMEM((HEADS_EACH, group_rows, HEAD_DIM), low),
                pltpu.VMEM((HEADS_EACH, group_rows, HEAD_DIM), low),
                pltpu.VMEM((HEAD_DIM, keys), low),
                pltpu.VMEM((HEAD_DIM, keys), low),
                pltpu.VMEM((RING, tok), jnp.int32),
                pltpu.VMEM((window, tok), full),
                pltpu.VMEM((window, tok), full),
                pltpu.VMEM((window, tok), low),
                pltpu.VMEM((window, tok), low),
                pltpu.VMEM((keys, HEAD_DIM), full),
                pltpu.VMEM((keys, HEAD_DIM), full),
                pltpu.VMEM((HEADS_EACH, 4, group_rows, HEAD_DIM), low),
                pltpu.VMEM((HEADS_EACH, 2, halo, HEAD_DIM), low),
                pltpu.VMEM((HEADS_EACH, 2, halo, HEAD_DIM), low),
                dma((HEADS_EACH, 4, RING)),
                dma((HEADS_EACH, 4, RING)),
                dma((HEADS_EACH, 2, REACH)),
                dma((HEADS_EACH, 2, REACH)),
                dma((HEADS_EACH, 2, REACH)),
                dma((HEADS_EACH, 2, REACH)),
                dma((2,)),
                dma((2,)),
                pltpu.SMEM(doc_lengths.shape, jnp.int32),
                dma(()),
                pltpu.SemaphoreType.REGULAR,
            ],
            compiler_params=pltpu.CompilerParams(
                collective_id=0, has_side_effects=True, vmem_limit_bytes=58 * 2**20
            ),
            cost_estimate=pl.CostEstimate(
                flops=flops, bytes_accessed=16 * tok * width, transcendentals=0
            ),
        )(doc_lengths, queries, key_rows, value_rows, out_grad)
        return pl.pallas_call(
            write_out,
            out_shape=[out] * 4,
            in_specs=[any_space],
            out_specs=[any_space] * 4,
            scratch_shapes=[dma((4,))],
            compiler_params=pltpu.CompilerParams(vmem_limit_bytes=2**20),
            cost_estimate=pl.CostEstimate(
                flops=0, bytes_accessed=16 * tok * width, transcendentals=0
            ),
        )(pltpu.with_memory_space_constraint(results, pltpu.VMEM))

    rows_spec = P(("dp", "blk"), None)
    return jax.shard_map(
        on_device,
        mesh=mesh,
        in_specs=(rows_spec,) * 4 + (P("dp"),),
        out_specs=(rows_spec,) * 4,
        check_vma=False,
    )
```
